256 devices in a mesh: wide: 32 (over y, z), hist: 8 (over x, core).
Axes of the slice: x: 4, y: 4, z: 8, core: 2. Of those that a mesh axis runs over, the one named last changes fastest.
Arguments:
- x_home: bfloat16 [262144, 256], P(('wide', 'hist')), may hold values from -6 to 6
- cotangent: bfloat16 [262144, 256], P(('wide', 'hist')), may hold values from -6 to 6
- owner: int32 [262144, 1], P(('wide', 'hist')), may hold values from 0 to 31; in each aligned block of 1024 rows (0 to 1023, 1024 to 2047, ...) at most 64 rows name the same one
- weights: bfloat16 [2, 256, 256], replicated, may hold values from -0.375 to 0.375
- history: bfloat16 [2, 8192, 256], P(None, 'hist'), may hold values from -6 to 6
- halo_ids: int32 [32, 8, 8, 64], P('wide', 'hist'), may hold values from 0 to 1023
- halo_count: int32 [32, 8, 8], P('wide', 'hist'), may hold values from 1 to 64, as said below
- tile_rows: int32 [32, 8, 96], P('wide', 'hist'), may hold values from 0 to 15
- tile_cols: int32 [32, 8, 96], P('wide', 'hist'), may hold values from 0 to 19
- tile_count: int32 [32, 8], P('wide', 'hist'), may hold values from 32 to 96, as said below
- tile_vals: bfloat16 [32, 8, 96, 128, 128], P('wide', 'hist'), may hold values from -0.21875 to 0.21875
Outputs:
- second_out: bfloat16 [262144, 256], P(('wide', 'hist'))
- weight_grads: float32 [2, 256, 256], replicated
The draws below stay inside these ranges and needn't reach their ends.
Inputs may be any that keep to these rules, and one draw needn't show every extreme that they name: At most 64 rows of one device name the same owner; in every draw some device sends exactly 64 rows to one owner. `halo_ids`: row numbers within one table shard; slots at or past the count are ignored. `halo_count`: some owner uses all 64 slots of some shard in every draw. `tile_cols`: column tiles 16 and above are the halo's. `tile_count`: some owner uses all 96 slots in every draw.
All inputs are finite; a program needn't handle non-finite values.
Results may differ from the reference program's by a relative error of at most 0.0055.
Values may be sent and summed in bfloat16 or wider, within the bound.
No kernel may reach another device: no remote copies, remote signals or barrier semaphores. Data moves between devices by JAX's collectives and lax.ppermute only.
A program may use at most 128 MiB of HBM per device.

```python
import math
import jax
import jax.numpy as jnp
import numpy as np
from jax import lax

D = 256
TILE = 128
TPR = 6
ROWS_DEV = 1024
HALO_DEV = 512
HIST_DEV = 1024
CAP = 64
HCAP = 64
RT = 16
CT = 20
NT_MAX = 96
NODES = 262144
HIST_ROWS = 8192
N_WIDE = 32
N_HIST = 8


def forced_top(key, shape, low, top):
    first, second = jax.random.split(key)
    values = jax.random.randint(first, shape, low, top + 1)
    total = 1
    for extent in shape:
        total = total * extent
    spot = jax.random.randint(second, (), 0, total)
    flat = jnp.where(jnp.arange(total) == spot, top, values.reshape(-1))
    return flat.reshape(shape).astype(jnp.int32)


def draw_halo_count(key, part):
    key = jax.random.fold_in(key, 11)
    return forced_top(key, (N_WIDE, N_HIST, N_HIST), 1, HCAP)


def draw_tile_count(key, part):
    key = jax.random.fold_in(key, 23)
    return forced_top(key, (N_WIDE, N_HIST), NT_MAX // 3, NT_MAX)


def set_ends(drawn, key, least, largest):
    longest = drawn.shape.index(max(drawn.shape))
    spots = []
    for shift in (0, 1):
        where = [jax.random.randint(jax.random.fold_in(key, axis), (), 0, length) for axis, length in enumerate(drawn.shape)]
        where[longest] = (where[longest] + shift) % drawn.shape[longest]
        spots.append(tuple(where))
    return drawn.at[spots[0]].set(least).at[spots[1]].set(largest)


def shard_levels(stream_key, shape, cuts, low, high):
    factor_of, own = 1.0, jax.random.fold_in(stream_key, 6)
    for axis_at, blocks in cuts:
        steps = jnp.exp(jax.random.uniform(jax.random.fold_in(own, axis_at), (blocks,), jnp.float32, low / len(cuts), high / len(cuts)))
        factor_of = factor_of * jnp.repeat(steps, shape[axis_at] // blocks).reshape([-1 if axis == axis_at else 1 for axis in range(len(shape))])
    return factor_of


def shared_out(stream_key, own, number, rows, count, top, most, skew):
    sequence = jax.random.permutation(stream_key, count)
    heavy_load, common = portions_of(count, rows * top, most, skew, True), portions_of(count, rows * top, most, skew, False)
    places = jnp.arange(count)

    def named(sizes, offset_by):
        used = int((sizes > 0).sum())
        fixed = max(1, used // 4)
        moved = fixed + (places - fixed + offset_by * (used - fixed)) % max(1, count - fixed)
        return jnp.zeros((count,), jnp.int32).at[sequence[jnp.where(places < fixed, places, moved)]].set(jnp.asarray(sizes, jnp.int32))

    sizes = jnp.where(number % 4 == 0, named(heavy_load, number // 4), named(common, number - number // 4 - 1))
    mixed = jax.random.permutation(jax.random.fold_in(own, 3), count)
    donor, taker = mixed[0:count // 2 * 2:2], mixed[1:count // 2 * 2:2]
    slack = jnp.minimum(sizes[donor] - 1, most - sizes[taker]) // 2
    slack = jnp.where((donor == sequence[0]) | (taker == sequence[0]) | (sizes[taker] == 0), 0, jnp.maximum(slack, 0))
    moved = jax.random.randint(jax.random.fold_in(own, 4), (count // 2,), 0, 1 << 20) % (slack + 1)
    sizes = sizes.at[donor].add(-moved).at[taker].add(moved)
    items = jnp.searchsorted(jnp.cumsum(sizes), jnp.arange(rows * top), side="right").astype(jnp.int32)
    listing = items.reshape(top, rows).T
    listing = listing[jax.random.permutation(jax.random.fold_in(own, 1), rows)]
    offset_by = jax.random.randint(jax.random.fold_in(own, 2), (rows, 1), 0, top)
    return jnp.take_along_axis(listing, (jnp.arange(top)[None, :] + offset_by) % top, axis=1)


def portions_of(number_of, total, limit, skew, full):
    loads = [(1 << 20) // math.isqrt(rank ** skew) + 1 for rank in range(1, number_of + 1)]
    largest = limit if full else min(limit, max(-(-total // number_of), total * loads[0] // sum(loads)))
    least = 1 if total - largest >= number_of - 1 else 0
    holding, surplus = [largest] + [least] * (number_of - 1), total - largest - least * (number_of - 1)
    while surplus > 0:
        candidates = [i for i in range(1, number_of) if holding[i] < largest] or [i for i in range(1, number_of) if holding[i] < limit]
        whole, left = sum([loads[i] for i in candidates]), surplus
        for i in candidates:
            extra = min(limit - holding[i], max(1, left * loads[i] // whole), surplus)
            holding[i] = holding[i] + extra
            surplus = surplus - extra
    return np.array(holding)


def centred(key, dims, scale, limit, cuts=(), kind=jnp.bfloat16):
    level = shard_levels(key, dims, cuts, -0.22, 0.18) if cuts else 1.0
    array = jax.random.normal(key, dims, jnp.float32) * scale * level
    return jnp.minimum(jnp.maximum(array, -limit), limit).astype(kind)


def setup_inputs(seed: int = 0) -> dict:
    key_list = jax.random.split(jax.random.key(seed), 12)
    x_home = centred(key_list[0], (NODES, D), 1.0, 6.0, ((0, 256),))
    cotangent = centred(key_list[1], (NODES, D), 1.0, 6.0, ((0, 256),))
    owner_keys = jax.random.split(jax.random.fold_in(key_list[2], 1), NODES // ROWS_DEV)
    owner_turns = jax.random.permutation(jax.random.fold_in(key_list[2], 3), NODES // ROWS_DEV)
    owner = jax.vmap(lambda own, number: shared_out(jax.random.fold_in(key_list[2], 2), own, number, ROWS_DEV, N_WIDE, 1, CAP, 1))(owner_keys, owner_turns).reshape((NODES, 1))
    weights = centred(key_list[3], (2, D, D), D ** -0.5, 0.375)
    history = centred(key_list[4], (2, HIST_ROWS, D), 1.0, 6.0, ((1, 8),))
    halo_ids = set_ends(jax.random.randint(key_list[5], (N_WIDE, N_HIST, N_HIST, HCAP), 0, HIST_DEV), jax.random.fold_in(key_list[5], 1), 0, HIST_DEV - 1).astype(jnp.int32)
    halo_count = draw_halo_count(jax.random.fold_in(key_list[11], 71), 0)
    tile_rows = set_ends(jax.random.randint(key_list[7], (N_WIDE, N_HIST, NT_MAX), 0, RT), jax.random.fold_in(key_list[7], 1), 0, RT - 1).astype(jnp.int32)
    tile_cols = set_ends(jax.random.randint(key_list[8], (N_WIDE, N_HIST, NT_MAX), 0, CT), jax.random.fold_in(key_list[8], 1), 0, CT - 1).astype(jnp.int32)
    tile_count = draw_tile_count(jax.random.fold_in(key_list[11], 71), 0)
    tile_vals = centred(key_list[10], (N_WIDE, N_HIST, NT_MAX, TILE, TILE), (TPR * TILE) ** -0.5, 0.21875, ((0, 32), (1, 8)))
    return dict(x_home=x_home, cotangent=cotangent, owner=owner, weights=weights, history=history, halo_ids=halo_ids, halo_count=halo_count, tile_rows=tile_rows, tile_cols=tile_cols, tile_count=tile_count, tile_vals=tile_vals)


ALPHA = 0.1
BETAS = (math.log(1.5), math.log(1.25))


def slope(pre):
    sig = jax.nn.sigmoid(pre)
    return sig * (1.0 + pre * (1.0 - sig))


def spread(ext, vals, cols, select_rows):
    tiles = ext.reshape(-1, TILE, D)[cols].astype(jnp.float32)
    prod = jnp.einsum("kij,kjd->kid", vals.astype(jnp.float32), tiles, precision=lax.Precision.HIGHEST)
    return jnp.einsum("kr,kid->rid", select_rows, prod, precision=lax.Precision.HIGHEST).reshape(-1, D)


def local_pass(ws_x, ws_cot, valid, halo, weights, rows, cols, count, vals):
    work = ws_x.shape[0]
    live = (jnp.arange(NT_MAX) < count).astype(jnp.float32)
    select_rows = (rows[:, None] == jnp.arange(work // TILE)[None, :]).astype(jnp.float32) * live[:, None]
    select_back = (cols[:, None] == jnp.arange(work // TILE)[None, :]).astype(jnp.float32) * live[:, None]
    h0f = ws_x.astype(jnp.float32)
    keep = valid.astype(jnp.float32)[:, None]
    prev = ws_x
    saved = []
    for layer in range(2):
        ext = jnp.concatenate([prev, halo[layer]], axis=0)
        support = spread(ext, vals, cols, select_rows)
        mixed = (1.0 - ALPHA) * support + ALPHA * h0f
        mixed_b = mixed.astype(jnp.bfloat16)
        pre = (1.0 - BETAS[layer]) * mixed + BETAS[layer] * jnp.dot(mixed_b, weights[layer], preferred_element_type=jnp.float32)
        prev = (jax.nn.silu(pre) * keep).astype(jnp.bfloat16)
        saved.append((mixed_b, pre))
    grad_two = ws_cot.astype(jnp.float32) * keep * slope(saved[1][1])
    grad_two_b = grad_two.astype(jnp.bfloat16)
    weight_two = BETAS[1] * jnp.dot(saved[1][0].T, grad_two_b, preferred_element_type=jnp.float32)
    grad_mix = (1.0 - BETAS[1]) * grad_two + BETAS[1] * jnp.dot(grad_two_b, weights[1].T, preferred_element_type=jnp.float32)
    grad_mix_b = grad_mix.astype(jnp.bfloat16)
    gathered = grad_mix_b.reshape(-1, TILE, D)[rows].astype(jnp.float32)
    back_prod = jnp.einsum("kij,kid->kjd", vals.astype(jnp.float32), gathered, precision=lax.Precision.HIGHEST)
    back = jnp.einsum("kc,kjd->cjd", select_back, back_prod, precision=lax.Precision.HIGHEST).reshape(-1, D)
    grad_one = (1.0 - ALPHA) * back * keep * slope(saved[0][1])
    grad_one_b = grad_one.astype(jnp.bfloat16)
    weight_one = BETAS[0] * jnp.dot(saved[0][0].T, grad_one_b, preferred_element_type=jnp.float32)
    return prev, jnp.stack([weight_one, weight_two])


def reference(x_home, cotangent, owner, weights, history, halo_ids, halo_count, tile_rows, tile_cols, tile_count, tile_vals):
    cap = 2 * ROWS_DEV // N_WIDE
    work = 2 * ROWS_DEV
    own = owner[:, 0].reshape(N_WIDE, N_HIST, ROWS_DEV).astype(jnp.int32)
    onehot = (own[..., None] == jnp.arange(N_WIDE, dtype=jnp.int32)[None, None, None, :]).astype(jnp.int32)
    rank = jnp.sum((jnp.cumsum(onehot, axis=2) - onehot) * onehot, axis=-1).astype(jnp.int32)
    source = (jnp.arange(N_WIDE, dtype=jnp.int32)[:, None, None] * cap + rank).astype(jnp.int32)
    hold = jnp.broadcast_to(jnp.arange(N_HIST, dtype=jnp.int32)[None, :, None], own.shape).astype(jnp.int32)
    empty = jnp.zeros((N_WIDE, N_HIST, work, D), jnp.bfloat16)
    ws_x = empty.at[own, hold, source].set(x_home.reshape(N_WIDE, N_HIST, ROWS_DEV, D))
    ws_cot = empty.at[own, hold, source].set(cotangent.reshape(N_WIDE, N_HIST, ROWS_DEV, D))
    valid = jnp.zeros((N_WIDE, N_HIST, work), jnp.bfloat16).at[own, hold, source].set(jnp.ones(own.shape, jnp.bfloat16))
    global_ids = (jnp.arange(N_HIST, dtype=jnp.int32)[None, None, :, None] * HIST_DEV + halo_ids).astype(jnp.int32)
    live_halo = jnp.arange(HCAP)[None, None, None, :] < halo_count[..., None]
    flat = N_WIDE * N_HIST

    def visit(total, item):
        xw, cw, vw, gid, live, rows, cols, count, vals = item
        halo = jnp.where(live[None, :, None], history[:, gid], jnp.zeros((), jnp.bfloat16))
        out, grads = local_pass(xw, cw, vw, halo, weights, rows, cols, count, vals)
        return total + grads, out

    items = (ws_x.reshape(flat, work, D), ws_cot.reshape(flat, work, D), valid.reshape(flat, work),
             global_ids.reshape(flat, HALO_DEV), live_halo.reshape(flat, HALO_DEV),
             tile_rows.reshape(flat, NT_MAX), tile_cols.reshape(flat, NT_MAX), tile_count.reshape(flat),
             tile_vals.reshape(flat, NT_MAX, TILE, TILE))
    grads, outs = lax.scan(visit, jnp.zeros((2, D, D), jnp.float32), items)
    outs = outs.reshape(N_WIDE, N_HIST, work, D)
    second_out = outs[own, hold, source].reshape(NODES, D)
    return second_out, grads
```

```python
import math

import jax
import jax.numpy as jnp
from jax import lax
from jax.experimental import pallas as pl
from jax.experimental.pallas import tpu as pltpu
from jax.sharding import PartitionSpec as P

ALPHA = 0.1
BETAS = (math.log(1.5), math.log(1.25))
TILE = 128
CAP = 64
HCAP = 64
MARK = 1024.0
LIMIT = 512.0
BF16 = jnp.bfloat16
F32 = jnp.float32
MIB = 1 << 20


def vmem(count):
    return [pl.BlockSpec(memory_space=pltpu.VMEM)] * count


def smem(count):
    return [pl.BlockSpec(memory_space=pltpu.SMEM)] * count


def cost(flops, moved):
    return pl.CostEstimate(flops=flops, bytes_accessed=moved, transcendentals=0)


def dot(a, b):
    return jnp.dot(a, b, preferred_element_type=F32)


def dot_rows(a, b):
    return lax.dot_general(a, b, (((0,), (0,)), ((), ())), preferred_element_type=F32)


def route_body(n_wide, own_ref, x_ref, cot_ref, send_ref, place_ref):
    rows_here = own_ref.shape[1]
    width = x_ref.shape[1]
    blocks = rows_here // 128
    own = own_ref[...]
    ids = lax.broadcasted_iota(jnp.int32, (n_wide, 128), 0)
    hot = [(own[:, 128 * b : 128 * (b + 1)] == ids).astype(F32) for b in range(blocks)]
    lower = lax.broadcasted_iota(jnp.int32, (128, 128), 0)
    upper = lax.broadcasted_iota(jnp.int32, (128, 128), 1)
    earlier = (lower < upper).astype(F32).astype(BF16)
    inside = dot(jnp.concatenate(hot, axis=0).astype(BF16), earlier)
    before = jnp.zeros((n_wide, 1), F32)
    ranks = []
    for b in range(blocks):
        seen = inside[n_wide * b : n_wide * (b + 1)] + before
        ranks.append(jnp.sum(seen * hot[b], axis=0, keepdims=True))
        before = before + jnp.sum(hot[b], axis=1, keepdims=True)
    place = own * CAP + jnp.concatenate(ranks, axis=1).astype(jnp.int32)
    place_ref[...] = place
    step = 256
    base = lax.broadcasted_iota(jnp.int32, (step, rows_here), 0)
    for c in range(send_ref.shape[0] // step):
        hit = (base == place - c * step).astype(F32)
        held = jnp.max(hit, axis=1, keepdims=True)
        hit = hit.astype(BF16)
        x_part = jnp.where(held > 0.5, dot(hit, x_ref[...]), MARK)
        send_ref[pl.ds(c * step, step), :width] = x_part.astype(BF16)
        send_ref[pl.ds(c * step, step), width:] = dot(hit, cot_ref[...]).astype(BF16)


def prepare_body(rows_ref, cols_ref, count_ref, place_ref, vals_ref, adj_ref, column_ref, head, following):
    adj_ref[...] = jnp.zeros_like(adj_ref)
    count = count_ref[0]
    wide = adj_ref.shape[1] // TILE

    def clear(k, carry):
        head[rows_ref[k] * wide + cols_ref[k]] = -1
        return carry

    lax.fori_loop(0, count, clear, 0)

    def chain(i, carry):
        k = count - 1 - i
        cell = rows_ref[k] * wide + cols_ref[k]
        following[k] = head[cell]
        head[cell] = k
        return carry

    lax.fori_loop(0, count, chain, 0)

    def fill(k, carry):
        row, col = rows_ref[k], cols_ref[k]

        @pl.when(head[row * wide + col] == k)
        def _():
            def more(state):
                at, total = state
                return following[at], total + vals_ref[at].astype(F32)

            _, total = lax.while_loop(
                lambda state: state[0] >= 0, more, (following[k], vals_ref[k].astype(F32))
            )
            adj_ref[
                pl.ds(pl.multiple_of(row * TILE, TILE), TILE),
                pl.ds(pl.multiple_of(col * TILE, TILE), TILE),
            ] = total.astype(BF16)

        return carry

    lax.fori_loop(0, count, fill, 0)
    for b in range(place_ref.shape[1] // 128):
        part = place_ref[:, 128 * b : 128 * (b + 1)].astype(F32)
        column_ref[pl.ds(128 * b, 128), :] = jnp.transpose(jnp.broadcast_to(part, (128, 128)))


def pick_body(ids_ref, history_ref, *piece_refs):
    slots = ids_ref.shape[0]
    here = history_ref.shape[1]
    lane = lax.broadcasted_iota(jnp.int32, (slots, 128), 1)
    ids = ids_ref[...]
    hit = jnp.concatenate(
        [(ids - 128 * c == lane).astype(F32).astype(BF16) for c in range(here // 128)], axis=1
    )
    for layer in range(2):
        rows = dot(hit, history_ref[layer]).astype(BF16)
        for k, piece_ref in enumerate(piece_refs):
            piece_ref[pl.ds(layer * HCAP, HCAP), :] = rows[k * HCAP : (k + 1) * HCAP]


def forward_body(turn_ref, ws_ref, adj_ref, w_ref, *rest):
    n_hist = (len(rest) - 7)
    pieces = rest[:n_hist]
    out_ref, m1_ref, m2_ref, s1_ref, s2_ref, ext0, ext1 = rest[n_hist:]
    work, width = out_ref.shape
    turn = turn_ref[0]
    for layer, ext in enumerate((ext0, ext1)):
        for k, piece in enumerate(pieces):
            shard = lax.rem(turn + k, n_hist)
            at = pl.multiple_of(work + shard * HCAP, HCAP)
            ext[pl.ds(at, HCAP), :] = piece[pl.ds(layer * HCAP, HCAP), :]
    step = 512
    for b in range(work // step):
        part = pl.ds(b * step, step)
        got = ws_ref[part, :width].astype(F32)
        ext0[part, :] = jnp.where(got < LIMIT, got, 0.0).astype(BF16)
    for layer in range(2):
        ext, m_ref, s_ref = ((ext0, m1_ref, s1_ref), (ext1, m2_ref, s2_ref))[layer]
        beta = BETAS[layer]
        for b in range(work // step):
            part = pl.ds(b * step, step)
            support = dot(adj_ref[part, :], ext[...])
            mixed = (1.0 - ALPHA) * support + ALPHA * ext0[part, :].astype(F32)
            mixed_b = mixed.astype(BF16)
            m_ref[part, :] = mixed_b
            pre = (1.0 - beta) * mixed + beta * dot(mixed_b, w_ref[layer])
            sig = jax.nn.sigmoid(pre)
            keep = ws_ref[part, :width].astype(F32) < LIMIT
            new = jnp.where(keep, pre * sig, 0.0).astype(BF16)
            s_ref[part, :] = jnp.where(keep, sig * (1.0 + pre * (1.0 - sig)), 0.0)
            if layer == 0:
                ext1[part, :] = new
            else:
                out_ref[part, :] = new


def backward_body(ws_ref, adj_ref, w_ref, m1_ref, m2_ref, s1_ref, s2_ref, grads_ref, turned):
    work, width = m1_ref.shape
    step = 512
    beta = BETAS[1]
    total = jnp.zeros((width, width), F32)
    for b in range(work // step):
        part = pl.ds(b * step, step)
        grad_two = ws_ref[part, width:].astype(F32) * s2_ref[part, :]
        grad_two_b = grad_two.astype(BF16)
        total = total + dot_rows(m2_ref[part, :], grad_two_b)
        through = lax.dot_general(
            grad_two_b, w_ref[1], (((1,), (1,)), ((), ())), preferred_element_type=F32
        )
        grad_mix = (1.0 - beta) * grad_two + beta * through
        turned[:, pl.ds(b * step, step)] = jnp.transpose(grad_mix.astype(BF16))
    grads_ref[1] = BETAS[1] * total
    total = jnp.zeros((width, width), F32)
    for b in range(work // step):
        part = pl.ds(b * step, step)
        back = jnp.transpose(dot(turned[...], adj_ref[:, pl.ds(b * step, step)]))
        grad_one = (1.0 - ALPHA) * back * s1_ref[part, :]
        total = total + dot_rows(m1_ref[part, :], grad_one.astype(BF16))
    grads_ref[0] = BETAS[0] * total


def collect_body(column_ref, back_ref, out_ref):
    slots = back_ref.shape[0]
    step = 256
    lane = lax.broadcasted_iota(jnp.int32, (step, 128), 1).astype(F32)
    for b in range(out_ref.shape[0] // step):
        part = pl.ds(b * step, step)
        place = column_ref[part, :]
        hit = jnp.concatenate(
            [(place - 128.0 * c == lane).astype(F32).astype(BF16) for c in range(slots // 128)],
            axis=1,
        )
        out_ref[part, :] = dot(hit, back_ref[...]).astype(BF16)


def local(
    x_home,
    cotangent,
    owner,
    weights,
    history,
    halo_ids,
    halo_count,
    tile_rows,
    tile_cols,
    tile_count,
    tile_vals,
):
    n_wide = lax.axis_size("wide")
    n_hist = lax.axis_size("hist")
    turn = lax.axis_index("hist")
    rows_here, width = x_home.shape
    work = n_wide * CAP
    halo = n_hist * HCAP
    slots = tile_vals.shape[2]
    params = pltpu.CompilerParams(vmem_limit_bytes=48 * MIB)

    send, place = pl.pallas_call(
        lambda *refs: route_body(n_wide, *refs),
        out_shape=(
            jax.ShapeDtypeStruct((work, 2 * width), BF16),
            jax.ShapeDtypeStruct((1, rows_here), jnp.int32),
        ),
        in_specs=vmem(3),
        out_specs=tuple(vmem(2)),
        compiler_params=params,
        cost_estimate=cost(4 * work * rows_here * width, 3 * MIB),
        name="route",
    )(owner.reshape(1, rows_here), x_home, cotangent)
    ws = lax.all_to_all(
        send.reshape(n_wide, CAP, 2 * width), "wide", split_axis=0, concat_axis=0, tiled=True
    ).reshape(work, 2 * width)

    live = jnp.arange(HCAP)[None, :] < halo_count[0, 0][:, None]
    wanted = jnp.where(live, halo_ids[0, 0], -1)
    wanted, place = lax.optimization_barrier((wanted, place))
    wanted = lax.dynamic_slice_in_dim(jnp.concatenate([wanted, wanted]), turn, n_hist, axis=0)

    def shift(value, by):
        return lax.ppermute(value, "hist", [(i, (i + by) % n_hist) for i in range(n_hist)])

    asked = [wanted[0]] + [shift(wanted[k], k) for k in range(1, n_hist)]
    asked = jnp.broadcast_to(jnp.stack(asked).reshape(halo, 1), (halo, 128))
    picked = pl.pallas_call(
        pick_body,
        out_shape=tuple(jax.ShapeDtypeStruct((2 * HCAP, width), BF16) for _ in range(n_hist)),
        in_specs=vmem(2),
        out_specs=tuple(vmem(n_hist)),
        compiler_params=params,
        cost_estimate=cost(4 * halo * history.shape[1] * width, 2 * MIB),
        name="pick",
    )(asked, history)
    pieces = [picked[0]] + [shift(picked[k], n_hist - k) for k in range(1, n_hist)]

    adjacency, column = pl.pallas_call(
        prepare_body,
        out_shape=(
            jax.ShapeDtypeStruct((work, work + halo), BF16),
            jax.ShapeDtypeStruct((rows_here, 128), F32),
        ),
        in_specs=smem(3) + vmem(2),
        out_specs=tuple(vmem(2)),
        scratch_shapes=[
            pltpu.SMEM(((work // TILE) * ((work + halo) // TILE),), jnp.int32),
            pltpu.SMEM((slots,), jnp.int32),
        ],
        compiler_params=params,
        cost_estimate=cost(0, 24 * MIB),
        name="prepare",
    )(tile_rows[0, 0], tile_cols[0, 0], tile_count[0], place, tile_vals[0, 0])

    second, m1, m2, s1, s2 = pl.pallas_call(
        forward_body,
        out_shape=tuple(
            jax.ShapeDtypeStruct((work, width), kind) for kind in (BF16, BF16, BF16, F32, F32)
        ),
        in_specs=smem(1) + vmem(3 + n_hist),
        out_specs=tuple(vmem(5)),
        scratch_shapes=[pltpu.VMEM((work + halo, width), BF16)] * 2,
        compiler_params=params,
        cost_estimate=cost(4 * work * (work + halo + width) * width, 24 * MIB),
        name="forward",
    )(turn.reshape(1), ws, adjacency, weights, *pieces)
    returned = lax.all_to_all(
        second.reshape(n_wide, CAP, width), "wide", split_axis=0, concat_axis=0, tiled=True
    ).reshape(work, width)

    grads = pl.pallas_call(
        backward_body,
        out_shape=jax.ShapeDtypeStruct((2, width, width), F32),
        in_specs=vmem(7),
        out_specs=vmem(1)[0],
        scratch_shapes=[pltpu.VMEM((width, work), BF16)],
        compiler_params=params,
        cost_estimate=cost(2 * work * (work + 3 * width) * width, 20 * MIB),
        name="backward",
    )(ws, adjacency, weights, m1, m2, s1, s2)

    second_out = pl.pallas_call(
        collect_body,
        out_shape=jax.ShapeDtypeStruct((rows_here, width), BF16),
        in_specs=vmem(2),
        out_specs=vmem(1)[0],
        compiler_params=params,
        cost_estimate=cost(2 * work * rows_here * width, 2 * MIB),
        name="collect",
    )(column, returned)

    n_all = n_wide * n_hist
    lanes = 128
    chunk = 2 * width * width // n_all // lanes
    both = ("wide", "hist")
    parts = lax.all_to_all(
        grads.reshape(n_all, chunk, lanes), both, split_axis=0, concat_axis=0, tiled=True
    )
    mine = jnp.sum(parts, axis=0, keepdims=True)
    total = lax.all_to_all(
        jnp.broadcast_to(mine, (n_all, chunk, lanes)), both, split_axis=0, concat_axis=0, tiled=True
    ).reshape(2, width, width)
    return (second_out, total)


def solution(mesh):
    placed = (
        P(("wide", "hist"), None),
        P(("wide", "hist"), None),
        P(("wide", "hist"), None),
        P(),
        P(None, "hist", None),
        P("wide", "hist", None, None),
        P("wide", "hist", None),
        P("wide", "hist", None),
        P("wide", "hist", None),
        P("wide", "hist"),
        P("wide", "hist", None, None, None),
    )
    return jax.shard_map(
        local,
        mesh=mesh,
        in_specs=placed,
        out_specs=(P(("wide", "hist"), None), P()),
        check_vma=False,
    )
```

```python
import math

import jax
import jax.numpy as jnp
from jax import lax
from jax.experimental import pallas as pl
from jax.experimental.pallas import tpu as pltpu
from jax.sharding import Mesh
from jax.sharding import PartitionSpec as P

ALPHA = 0.1
BETAS = (math.log(1.5), math.log(1.25))
TILE = 128
CAP = 64
HCAP = 64
MARK = 1024.0
LIMIT = 512.0
BF16 = jnp.bfloat16
F32 = jnp.float32
MIB = 1 << 20
WIDE = ("y", "z")
HIST = ("x", "core")


def vmem(count):
    return [pl.BlockSpec(memory_space=pltpu.VMEM)] * count


def smem(count):
    return [pl.BlockSpec(memory_space=pltpu.SMEM)] * count


def params(limit):
    return pltpu.CompilerParams(vmem_limit_bytes=limit * MIB)


def cost(flops, moved):
    return pl.CostEstimate(flops=flops, bytes_accessed=moved, transcendentals=0)


def dot(a, b):
    return jnp.dot(a, b, preferred_element_type=F32)


def dot_rows(a, b):
    return lax.dot_general(a, b, (((0,), (0,)), ((), ())), preferred_element_type=F32)


def hits_of(place, start, step):
    slots = lax.broadcasted_iota(jnp.int32, (step, place.shape[1]), 0) + start
    return (slots == place).astype(F32)


def route_body(n_wide, own_ref, x_hbm, send_hbm, place_ref, x_all, send, load_sem, send_sem):
    load = pltpu.make_async_copy(x_hbm, x_all, load_sem)
    load.start()
    rows_here = own_ref.shape[1]
    blocks = rows_here // 128
    own = own_ref[...]
    ids = lax.broadcasted_iota(jnp.int32, (n_wide, 128), 0)
    hot = [(own[:, 128 * b : 128 * (b + 1)] == ids).astype(F32) for b in range(blocks)]
    lower = lax.broadcasted_iota(jnp.int32, (128, 128), 0)
    upper = lax.broadcasted_iota(jnp.int32, (128, 128), 1)
    earlier = (lower < upper).astype(F32).astype(BF16)
    inside = dot(jnp.concatenate(hot, axis=0).astype(BF16), earlier)
    before = jnp.zeros((n_wide, 1), F32)
    ranks = []
    for b in range(blocks):
        seen = inside[n_wide * b : n_wide * (b + 1)] + before
        ranks.append(jnp.sum(seen * hot[b], axis=0, keepdims=True))
        before = before + jnp.sum(hot[b], axis=1, keepdims=True)
    place = own * CAP + jnp.concatenate(ranks, axis=1).astype(jnp.int32)
    place_ref[...] = place
    load.wait()
    step = 256
    stores = []
    for c in range(send.shape[0] // step):
        part = pl.ds(c * step, step)
        hit = hits_of(place, c * step, step)
        held = jnp.max(hit, axis=1, keepdims=True)
        send[part, :] = jnp.where(held > 0.5, dot(hit.astype(BF16), x_all[...]), MARK).astype(BF16)
        store = pltpu.make_async_copy(send.at[part], send_hbm.at[part], send_sem.at[c])
        store.start()
        stores.append(store)
    for store in stores:
        store.wait()


def follow_body(place_ref, value_ref, send_ref):
    place = place_ref[...]
    step = 256
    for c in range(send_ref.shape[0] // step):
        hit = hits_of(place, c * step, step).astype(BF16)
        send_ref[pl.ds(c * step, step), :] = dot(hit, value_ref[...]).astype(BF16)


def prepare_body(rows_ref, cols_ref, count_ref, place_ref, vals_ref, adj_ref, column_ref, head, following):
    adj_ref[...] = jnp.zeros_like(adj_ref)
    count = count_ref[0]
    wide = adj_ref.shape[1] // TILE

    def clear(k, carry):
        head[rows_ref[k] * wide + cols_ref[k]] = -1
        return carry

    lax.fori_loop(0, count, clear, 0)

    def chain(i, carry):
        k = count - 1 - i
        cell = rows_ref[k] * wide + cols_ref[k]
        following[k] = head[cell]
        head[cell] = k
        return carry

    lax.fori_loop(0, count, chain, 0)

    def fill(k, carry):
        row, col = rows_ref[k], cols_ref[k]

        @pl.when(head[row * wide + col] == k)
        def _():
            def more(state):
                at, total = state
                return following[at], total + vals_ref[at].astype(F32)

            _, total = lax.while_loop(
                lambda state: state[0] >= 0, more, (following[k], vals_ref[k].astype(F32))
            )
            adj_ref[
                pl.ds(pl.multiple_of(row * TILE, TILE), TILE),
                pl.ds(pl.multiple_of(col * TILE, TILE), TILE),
            ] = total.astype(BF16)

        return carry

    lax.fori_loop(0, count, fill, 0)
    for b in range(place_ref.shape[1] // 128):
        part = place_ref[:, 128 * b : 128 * (b + 1)].astype(F32)
        column_ref[pl.ds(128 * b, 128), :] = jnp.transpose(jnp.broadcast_to(part, (128, 128)))


def pick_body(ids_ref, history_ref, own_ref, other_ref):
    slots = ids_ref.shape[0]
    here = history_ref.shape[1]
    lane = lax.broadcasted_iota(jnp.int32, (slots, 128), 1)
    ids = ids_ref[...]
    hit = jnp.concatenate(
        [(ids - 128 * c == lane).astype(F32).astype(BF16) for c in range(here // 128)], axis=1
    )
    size = own_ref.shape[0]
    for layer in range(2):
        rows = dot(hit, history_ref[layer]).astype(BF16)
        for side, ref in enumerate((own_ref, other_ref)):
            for k in range(size):
                at = (side * size + k) * HCAP
                ref[k, pl.ds(layer * HCAP, HCAP), :] = rows[at : at + HCAP]


def forward_body(size, turn_ref, ws_hbm, w_hbm, adj_hbm, *rest):
    pieces = rest[:size]
    out_hbm, m_hbm, s_hbm, adj, w, ws, ext0, ext1, m_all, s_all, out, acc0, acc1, load_sem, keep_sem = rest[size:]
    work, width = ws.shape
    step = acc0.shape[0]
    blocks = work // step
    rows = [pl.ds(b * step, step) for b in range(blocks)]
    first = [
        pltpu.make_async_copy(ws_hbm, ws, load_sem.at[0]),
        pltpu.make_async_copy(w_hbm, w, load_sem.at[1]),
    ]
    x, core = turn_ref[0], turn_ref[1]
    for layer, ext in enumerate((ext0, ext1)):
        for k, piece in enumerate(pieces):
            for side in range(2):
                shard = lax.rem(x + k, size) * 2 + lax.rem(core + side, 2)
                there = pl.ds(pl.multiple_of(work + shard * HCAP, HCAP), HCAP)
                here = pl.ds((2 * side + layer) * HCAP, HCAP)
                sem = load_sem.at[2 + (layer * size + k) * 2 + side]
                first.append(pltpu.make_async_copy(piece.at[here], ext.at[there], sem))
    for load in first:
        load.start()
    loads = {}
    for b, until in ((0, 1), (1, blocks // 2), (blocks // 2, blocks)):
        part = pl.ds(b * step, (until - b) * step)
        sem = load_sem.at[2 + 4 * size + len(loads)]
        loads[b] = pltpu.make_async_copy(adj_hbm.at[part], adj.at[part], sem)
        loads[b].start()
    for load in first:
        load.wait()
    for part in rows:
        got = ws[part, :].astype(F32)
        ext0[part, :] = jnp.where(got < LIMIT, got, 0.0).astype(BF16)
    stores = []

    def finish(layer, b, support):
        part = rows[b]
        beta = BETAS[layer]
        mixed = (1.0 - ALPHA) * support + ALPHA * ext0[part, :].astype(F32)
        mixed_b = mixed.astype(BF16)
        m_all[layer, part, :] = mixed_b
        pre = (1.0 - beta) * mixed + beta * dot(mixed_b, w[layer])
        sig = jax.nn.sigmoid(pre)
        keep = ws[part, :].astype(F32) < LIMIT
        raw = pre * sig
        new = jnp.where(keep, raw, 0.0).astype(BF16)
        s_all[layer, part, :] = jnp.where(keep, sig + raw * (1.0 - sig), 0.0)
        (ext1, out)[layer][part, :] = new
        moves = [(m_all.at[layer, part], m_hbm.at[layer, part]), (s_all.at[layer, part], s_hbm.at[layer, part])]
        if layer == 1:
            moves.insert(0, (out.at[part], out_hbm.at[part]))
        for kind, (here, there) in enumerate(moves):
            store = pltpu.make_async_copy(here, there, keep_sem.at[layer, kind, b])
            store.start()
            stores.append(store)

    accs = (acc0, acc1)
    for layer, ext in enumerate((ext0, ext1)):
        for b in range(blocks + 1):
            if b < blocks:
                if layer == 0 and b in loads:
                    loads[b].wait()
                accs[b % 2][...] = dot(adj[rows[b], :], ext[...])
            if b > 0:
                finish(layer, b - 1, accs[(b - 1) % 2][...])
    for store in stores:
        store.wait()


def backward_body(cot_ref, w_ref, adj_hbm, m_hbm, s_hbm, grads_ref, adj, m_all, s_all, turned, load_sem):
    work = m_all.shape[1]
    width = m_all.shape[2]
    step = 512
    blocks = work // step
    parts = [pl.ds(b * step, step) for b in range(blocks)]
    copies = [
        pltpu.make_async_copy(s_hbm.at[1], s_all.at[1], load_sem.at[0]),
        pltpu.make_async_copy(m_hbm.at[1], m_all.at[1], load_sem.at[1]),
    ]
    loads = [
        pltpu.make_async_copy(adj_hbm.at[:, part], adj.at[:, part], load_sem.at[4 + b])
        for b, part in enumerate(parts)
    ]
    late = [
        pltpu.make_async_copy(s_hbm.at[0], s_all.at[0], load_sem.at[2]),
        pltpu.make_async_copy(m_hbm.at[0], m_all.at[0], load_sem.at[3]),
    ]
    for copy in copies + loads[:1] + late + loads[1:]:
        copy.start()
    for copy in copies:
        copy.wait()
    beta = BETAS[1]
    total = jnp.zeros((width, width), F32)
    for part in parts:
        grad_two = cot_ref[part, :].astype(F32) * s_all[1, part, :]
        grad_two_b = grad_two.astype(BF16)
        total = total + dot_rows(m_all[1, part, :], grad_two_b)
        through = lax.dot_general(
            grad_two_b, w_ref[1], (((1,), (1,)), ((), ())), preferred_element_type=F32
        )
        grad_mix = (1.0 - beta) * grad_two + beta * through
        turned[:, part] = jnp.transpose(grad_mix.astype(BF16))
    grads_ref[1] = BETAS[1] * total
    for copy in late:
        copy.wait()
    total = jnp.zeros((width, width), F32)
    for b, part in enumerate(parts):
        loads[b].wait()
        back = jnp.transpose(dot(turned[...], adj[:, part]))
        grad_one = (1.0 - ALPHA) * back * s_all[0, part, :]
        total = total + dot_rows(m_all[0, part, :], grad_one.astype(BF16))
    grads_ref[0] = BETAS[0] * total


def collect_body(column_ref, back_ref, out_ref):
    slots = back_ref.shape[0]
    step = 256
    lane = lax.broadcasted_iota(jnp.int32, (step, 128), 1).astype(F32)
    for b in range(out_ref.shape[0] // step):
        part = pl.ds(b * step, step)
        place = column_ref[part, :]
        hit = jnp.concatenate(
            [(place - 128.0 * c == lane).astype(F32).astype(BF16) for c in range(slots // 128)],
            axis=1,
        )
        out_ref[part, :] = dot(hit, back_ref[...]).astype(BF16)


def local(
    x_home,
    cotangent,
    owner,
    weights,
    history,
    halo_ids,
    halo_count,
    tile_rows,
    tile_cols,
    tile_count,
    tile_vals,
):
    n_wide = lax.axis_size(WIDE)
    n_hist = lax.axis_size(HIST)
    rows_here, width = x_home.shape
    work = n_wide * CAP
    halo = n_hist * HCAP
    slots = tile_vals.shape[2]

    anywhere = pl.BlockSpec(memory_space=pl.ANY)
    x = lax.axis_index("x")
    core = lax.axis_index("core")
    size = lax.axis_size("x")

    def to_owners(value):
        value = value.reshape(n_wide, CAP, width)
        return lax.all_to_all(value, WIDE, split_axis=0, concat_axis=0, tiled=True).reshape(
            work, width
        )

    send, place = pl.pallas_call(
        lambda *refs: route_body(n_wide, *refs),
        out_shape=(
            pltpu.HBM((work, width), BF16),
            jax.ShapeDtypeStruct((1, rows_here), jnp.int32),
        ),
        in_specs=vmem(1) + [anywhere],
        out_specs=(anywhere, vmem(1)[0]),
        scratch_shapes=[
            pltpu.VMEM((rows_here, width), BF16),
            pltpu.VMEM((work, width), BF16),
            pltpu.SemaphoreType.DMA,
            pltpu.SemaphoreType.DMA((work // 256,)),
        ],
        compiler_params=params(56),
        cost_estimate=cost(2 * work * rows_here * width, 2 * MIB),
        name="route",
    )(owner.reshape(1, rows_here), x_home)
    ws = to_owners(send)

    send_cot = pl.pallas_call(
        follow_body,
        out_shape=jax.ShapeDtypeStruct((work, width), BF16),
        in_specs=vmem(2),
        out_specs=vmem(1)[0],
        compiler_params=params(16),
        cost_estimate=cost(2 * work * rows_here * width, 2 * MIB),
        name="follow",
    )(place, cotangent)
    adjacency, column = pl.pallas_call(
        prepare_body,
        out_shape=(
            pltpu.HBM((work, work + halo), BF16),
            jax.ShapeDtypeStruct((rows_here, 128), F32),
        ),
        in_specs=smem(3) + vmem(2),
        out_specs=tuple(vmem(2)),
        scratch_shapes=[
            pltpu.SMEM(((work // TILE) * ((work + halo) // TILE),), jnp.int32),
            pltpu.SMEM((slots,), jnp.int32),
        ],
        compiler_params=params(24),
        cost_estimate=cost(0, 24 * MIB),
        name="prepare",
    )(tile_rows[0, 0], tile_cols[0, 0], tile_count[0], place, tile_vals[0, 0])

    live = jnp.arange(HCAP)[None, :] < halo_count[0, 0][:, None]
    wanted = jnp.where(live, halo_ids[0, 0], -1)
    wanted, place = lax.optimization_barrier((wanted, place))
    wanted = wanted.reshape(size, 2, HCAP)
    wanted = lax.dynamic_slice_in_dim(jnp.concatenate([wanted, wanted]), x, size, axis=0)

    def shift(value, by):
        return lax.ppermute(value, "x", [(i, (i + by) % size) for i in range(size)])

    asked = jnp.stack([wanted[0]] + [shift(wanted[k], k) for k in range(1, size)])
    asked_own = jnp.where(core == 0, asked[:, 0], asked[:, 1])
    asked_other = swap_cores(jnp.where(core == 0, asked[:, 1], asked[:, 0]))
    asked = jnp.stack([asked_own, asked_other]).reshape(halo, 1)
    own, other = pl.pallas_call(
        pick_body,
        out_shape=(jax.ShapeDtypeStruct((size, 2 * HCAP, width), BF16),) * 2,
        in_specs=vmem(2),
        out_specs=tuple(vmem(2)),
        compiler_params=params(12),
        cost_estimate=cost(4 * halo * history.shape[1] * width, 2 * MIB),
        name="pick",
    )(jnp.broadcast_to(asked, (halo, 128)), history)
    send_cot, ws, adjacency, own, other = lax.optimization_barrier(
        (send_cot, ws, adjacency, own, other)
    )
    ws_cot = to_owners(send_cot)

    other = swap_cores(other)
    pieces = [jnp.concatenate([own[k], other[k]]) for k in range(size)]
    pieces = pieces[:1] + [shift(pieces[k], size - k) for k in range(1, size)]

    step = 256
    second, mixed, slopes = pl.pallas_call(
        lambda *refs: forward_body(size, *refs),
        out_shape=(
            pltpu.HBM((work, width), BF16),
            pltpu.HBM((2, work, width), BF16),
            pltpu.HBM((2, work, width), F32),
        ),
        in_specs=smem(1) + [anywhere] * (3 + size),
        out_specs=(anywhere,) * 3,
        scratch_shapes=[
            pltpu.VMEM((work, work + halo), BF16),
            pltpu.VMEM((2, width, width), BF16),
            pltpu.VMEM((work, width), BF16),
            pltpu.VMEM((work + halo, width), BF16),
            pltpu.VMEM((work + halo, width), BF16),
            pltpu.VMEM((2, work, width), BF16),
            pltpu.VMEM((2, work, width), F32),
            pltpu.VMEM((work, width), BF16),
            pltpu.VMEM((step, width), F32),
            pltpu.VMEM((step, width), F32),
            pltpu.SemaphoreType.DMA((5 + 4 * size,)),
            pltpu.SemaphoreType.DMA((2, 3, work // step)),
        ],
        compiler_params=params(56),
        cost_estimate=cost(4 * work * (work + halo + width) * width, 24 * MIB),
        name="forward",
    )(jnp.stack([x, core]).astype(jnp.int32), ws, weights, adjacency, *pieces)
    second, ws_cot = lax.optimization_barrier((second, ws_cot))
    returned = to_owners(second)

    grads = pl.pallas_call(
        backward_body,
        out_shape=jax.ShapeDtypeStruct((2, width, width), F32),
        in_specs=vmem(2) + [anywhere] * 3,
        out_specs=vmem(1)[0],
        scratch_shapes=[
            pltpu.VMEM((work, work), BF16),
            pltpu.VMEM((2, work, width), BF16),
            pltpu.VMEM((2, work, width), F32),
            pltpu.VMEM((width, work), BF16),
            pltpu.SemaphoreType.DMA((8,)),
        ],
        compiler_params=params(56),
        cost_estimate=cost(2 * work * (work + 3 * width) * width, 20 * MIB),
        name="backward",
    )(ws_cot, weights, adjacency, mixed, slopes)

    grads, returned = reduce_rows(grads), returned
    grads, returned = lax.optimization_barrier((grads, returned))
    second_out = pl.pallas_call(
        collect_body,
        out_shape=jax.ShapeDtypeStruct((rows_here, width), BF16),
        in_specs=vmem(2),
        out_specs=vmem(1)[0],
        compiler_params=params(24),
        cost_estimate=cost(2 * work * rows_here * width, 2 * MIB),
        name="collect",
    )(column, returned)
    mine = sum_wide(grads, n_wide)
    mine, second_out = lax.optimization_barrier((mine, second_out))
    return (second_out, spread(mine))


def swap_cores(value):
    return lax.ppermute(value, "core", [(0, 1), (1, 0)])


def reduce_rows(grads):
    core = lax.axis_index("core")
    kept = jnp.where(core == 0, grads[0], grads[1])
    given = jnp.where(core == 0, grads[1], grads[0])
    kept = kept + swap_cores(given)
    size = lax.axis_size("x")
    quarter = kept.shape[0] // size
    x = lax.axis_index("x")

    def rows_of(index):
        return lax.dynamic_slice_in_dim(kept, lax.rem(index, size) * quarter, quarter, axis=0)

    total = rows_of(x)
    for k in range(1, size):
        total = total + lax.ppermute(
            rows_of(x + k), "x", [(i, (i + k) % size) for i in range(size)]
        )
    return total


def sum_wide(part, n_wide):
    rows, width = part.shape
    some = rows // n_wide
    parts = lax.all_to_all(
        part.reshape(n_wide, some, width), WIDE, split_axis=0, concat_axis=0, tiled=True
    )
    return jnp.sum(parts, axis=0, keepdims=True)


def spread(mine):
    _, some, width = mine.shape
    every = ("x",) + WIDE
    n_every = lax.axis_size(every)
    own = lax.all_to_all(
        jnp.broadcast_to(mine, (n_every, some, width)),
        every,
        split_axis=0,
        concat_axis=0,
        tiled=True,
    ).reshape(n_every * some, width)
    other = swap_cores(own)
    core = lax.axis_index("core")
    return jnp.stack([jnp.where(core == 0, own, other), jnp.where(core == 0, other, own)])


def solution(mesh):
    sizes = (4, mesh.shape["wide"] // 4, mesh.shape["hist"] // 2, 2)
    split = Mesh(mesh.devices.reshape(sizes), WIDE + HIST)
    rows = P(WIDE + HIST, None)
    placed = (
        rows,
        rows,
        rows,
        P(),
        P(None, HIST, None),
        P(WIDE, HIST, None, None),
        P(WIDE, HIST, None),
        P(WIDE, HIST, None),
        P(WIDE, HIST, None),
        P(WIDE, HIST),
        P(WIDE, HIST, None, None, None),
    )
    return jax.shard_map(
        local,
        mesh=split,
        in_specs=placed,
        out_specs=(rows, P()),
        check_vma=False,
    )
```

```python
import math

import jax
import jax.numpy as jnp
from jax import lax
from jax.experimental import pallas as pl
from jax.experimental.pallas import tpu as pltpu
from jax.sharding import Mesh
from jax.sharding import PartitionSpec as P

ALPHA = 0.1
BETAS = (math.log(1.5), math.log(1.25))
TILE = 128
CAP = 64
HCAP = 64
MARK = 1024.0
LIMIT = 512.0
BF16 = jnp.bfloat16
F32 = jnp.float32
MIB = 1 << 20
WIDE = ("y", "z")
HIST = ("x", "core")


def vmem(count):
    return [pl.BlockSpec(memory_space=pltpu.VMEM)] * count


def smem(count):
    return [pl.BlockSpec(memory_space=pltpu.SMEM)] * count


def params(limit):
    return pltpu.CompilerParams(vmem_limit_bytes=limit * MIB)


def cost(flops, moved):
    return pl.CostEstimate(flops=flops, bytes_accessed=moved, transcendentals=0)


def in_hbm(value):
    return pltpu.with_memory_space_constraint(value, pltpu.HBM)


def dot(a, b):
    return jnp.dot(a, b, preferred_element_type=F32)


def dot_rows(a, b):
    return lax.dot_general(a, b, (((0,), (0,)), ((), ())), preferred_element_type=F32)


def hits_of(place, start, step):
    slots = lax.broadcasted_iota(jnp.int32, (step, place.shape[1]), 0) + start
    return (slots == place).astype(F32)


def route_body(n_wide, own_ref, x_hbm, send_hbm, place_ref, x_all, send, load_sem, send_sem):
    load = pltpu.make_async_copy(x_hbm, x_all, load_sem)
    load.start()
    rows_here = own_ref.shape[1]
    blocks = rows_here // 128
    own = own_ref[...]
    hot = (own == lax.broadcasted_iota(jnp.int32, (n_wide, rows_here), 0)).astype(F32)
    hot_b = hot.astype(BF16)
    lower = lax.broadcasted_iota(jnp.int32, (128, 128), 0)
    upper = lax.broadcasted_iota(jnp.int32, (128, 128), 1)
    earlier = (lower < upper).astype(F32).astype(BF16)
    parts = [slice(128 * b, 128 * (b + 1)) for b in range(blocks)]
    inside = dot(jnp.concatenate([hot_b[:, part] for part in parts], axis=0), earlier)
    before = jnp.zeros((n_wide, 1), F32)
    ranks = []
    for b, part in enumerate(parts):
        seen = inside[n_wide * b : n_wide * (b + 1)] + before
        ranks.append(jnp.sum(seen * hot[:, part], axis=0, keepdims=True))
        before = before + jnp.sum(hot[:, part], axis=1, keepdims=True)
    rank = jnp.concatenate(ranks, axis=1)
    place_ref[...] = own * CAP + rank.astype(jnp.int32)
    by_rank = (rank == lax.broadcasted_iota(jnp.int32, (CAP, rows_here), 0).astype(F32)).astype(F32)
    by_rank = by_rank.astype(BF16)
    slot = lax.broadcasted_iota(jnp.int32, (CAP, 1), 0).astype(F32)
    load.wait()
    peers = 8
    step = peers * CAP
    stores = []
    for c in range(n_wide // peers):
        part = pl.ds(c * step, step)
        group = range(c * peers, (c + 1) * peers)
        hit = jnp.concatenate([by_rank * hot_b[o : o + 1, :] for o in group], axis=0)
        held = jnp.concatenate([slot < before[o : o + 1, :] for o in group], axis=0)
        send[part, :] = jnp.where(held, dot(hit, x_all[...]), MARK).astype(BF16)
        store = pltpu.make_async_copy(send.at[part], send_hbm.at[part], send_sem.at[c])
        store.start()
        stores.append(store)
    for store in stores:
        store.wait()


def prepare_body(
    rows_ref, cols_ref, count_ref, place_ref, vals_hbm, cot_hbm, adj_hbm, send_hbm, column_ref,
    adj, vals, cot, send, head, following, row_head, row_next, load_sem, adj_sem, send_sem,
):
    loads = (
        pltpu.make_async_copy(vals_hbm, vals, load_sem.at[0]),
        pltpu.make_async_copy(cot_hbm, cot, load_sem.at[1]),
    )
    for load in loads:
        load.start()
    count = count_ref[0]
    n_rows, wide = adj.shape[0] // TILE, adj.shape[1] // TILE
    for r in range(n_rows):
        row_head[r] = -1

    def clear(k, carry):
        head[rows_ref[k] * wide + cols_ref[k]] = -1
        return carry

    lax.fori_loop(0, count, clear, 0)

    def chain(i, carry):
        k = count - 1 - i
        row = rows_ref[k]
        cell = row * wide + cols_ref[k]
        following[k] = head[cell]
        head[cell] = k
        row_next[k] = row_head[row]
        row_head[row] = k
        return carry

    lax.fori_loop(0, count, chain, 0)
    loads[0].wait()

    def row_copy(r):
        part = pl.ds(pl.multiple_of(r * TILE, TILE), TILE)
        return pltpu.make_async_copy(adj.at[part], adj_hbm.at[part], adj_sem.at[r])

    def fill(r, carry):
        part = pl.ds(pl.multiple_of(r * TILE, TILE), TILE)
        adj[part, :] = jnp.zeros((TILE, adj.shape[1]), BF16)

        def place_tile(k):
            col = cols_ref[k]

            @pl.when(head[r * wide + col] == k)
            def _():
                def more(state):
                    at, total = state
                    return following[at], total + vals[at].astype(F32)

                _, total = lax.while_loop(
                    lambda state: state[0] >= 0, more, (following[k], vals[k].astype(F32))
                )
                adj[part, pl.ds(pl.multiple_of(col * TILE, TILE), TILE)] = total.astype(BF16)

            return row_next[k]

        lax.while_loop(lambda k: k >= 0, place_tile, row_head[r])
        row_copy(r).start()
        return carry

    lax.fori_loop(0, n_rows, fill, 0)
    loads[1].wait()
    place = place_ref[...]
    step = 512
    stores = []
    for c in range(send.shape[0] // step):
        part = pl.ds(c * step, step)
        hit = hits_of(place, c * step, step).astype(BF16)
        send[part, :] = dot(hit, cot[...]).astype(BF16)
        store = pltpu.make_async_copy(send.at[part], send_hbm.at[part], send_sem.at[c])
        store.start()
        stores.append(store)
    for b in range(place.shape[1] // 128):
        part = place[:, 128 * b : 128 * (b + 1)].astype(F32)
        column_ref[pl.ds(128 * b, 128), :] = jnp.transpose(jnp.broadcast_to(part, (128, 128)))
    for store in stores:
        store.wait()

    def drain(r, carry):
        row_copy(r).wait()
        return carry

    lax.fori_loop(0, n_rows, drain, 0)


def pick_body(ids_ref, history_ref, *block_refs):
    slots = ids_ref.shape[0]
    here = history_ref.shape[1]
    lane = lax.broadcasted_iota(jnp.int32, (slots, 128), 1)
    ids = ids_ref[...]
    hit = jnp.concatenate(
        [(ids - 128 * c == lane).astype(F32).astype(BF16) for c in range(here // 128)], axis=1
    )
    size = len(block_refs)
    for layer in range(2):
        rows = dot(hit, history_ref[layer]).astype(BF16)
        for side in range(2):
            for k, ref in enumerate(block_refs):
                at = (side * size + k) * HCAP
                ref[pl.ds((2 * side + layer) * HCAP, HCAP), :] = rows[at : at + HCAP]


def forward_body(size, x_ref, core_ref, ws_hbm, w_hbm, adj_hbm, *rest):
    pieces = rest[:size], rest[size : 2 * size]
    out_hbm, m_hbm, s_hbm, adj, w, ws, ext0, ext1, m_all, s_all, out, acc0, acc1, load_sem, keep_sem = rest[2 * size :]
    work, width = ws.shape
    step = acc0.shape[0]
    blocks = work // step
    rows = [pl.ds(b * step, step) for b in range(blocks)]
    x, core = x_ref[0], core_ref[0]
    first = pltpu.make_async_copy(ws_hbm, ws, load_sem.at[0])
    first.start()
    loads = {}

    def load_rows(b, until):
        part = pl.ds(b * step, (until - b) * step)
        sem = load_sem.at[2 + 4 * size + len(loads)]
        loads[b] = pltpu.make_async_copy(adj_hbm.at[part], adj.at[part], sem)
        loads[b].start()

    def load_halo(layer, ext):
        copies = []
        for k in range(size):
            for side in range(2):
                shard = lax.rem(x + k, size) * 2 + lax.rem(core + side, 2)
                there = pl.ds(pl.multiple_of(work + shard * HCAP, HCAP), HCAP)
                here = pl.ds((2 * side + layer) * HCAP, HCAP)
                sem = load_sem.at[2 + (layer * size + k) * 2 + side]
                copies.append(pltpu.make_async_copy(pieces[side][k].at[here], ext.at[there], sem))
                copies[-1].start()
        return copies

    load_rows(0, 1)
    halos = [load_halo(0, ext0)]
    load_rows(1, 4)
    weight = pltpu.make_async_copy(w_hbm, w, load_sem.at[1])
    weight.start()
    load_rows(4, blocks)
    halos.append(load_halo(1, ext1))
    first.wait()
    for part in rows:
        got = ws[part, :].astype(F32)
        ext0[part, :] = jnp.where(got < LIMIT, got, 0.0).astype(BF16)
    for copy in halos[0]:
        copy.wait()
    weight.wait()
    stores = []

    def store(here, there, *at):
        copy = pltpu.make_async_copy(here, there, keep_sem.at[*at])
        copy.start()
        stores.append(copy)

    def keep(layer, b):
        part = rows[b]
        store(m_all.at[layer, part], m_hbm.at[layer, part], layer, 0, b)
        store(s_all.at[layer, part], s_hbm.at[layer, part], layer, 1, b)

    def finish(layer, b, support):
        part = rows[b]
        beta = BETAS[layer]
        mixed = (1.0 - ALPHA) * support + ALPHA * ext0[part, :].astype(F32)
        mixed_b = mixed.astype(BF16)
        m_all[layer, part, :] = mixed_b
        pre = (1.0 - beta) * mixed + beta * dot(mixed_b, w[layer])
        sig = jax.nn.sigmoid(pre)
        valid = ws[part, :].astype(F32) < LIMIT
        raw = pre * sig
        new = jnp.where(valid, raw, 0.0).astype(BF16)
        s_all[layer, part, :] = jnp.where(valid, sig + raw * (1.0 - sig), 0.0)
        (ext1, out)[layer][part, :] = new
        if layer == 1:
            store(out.at[part], out_hbm.at[part], 1, 2, b)
        keep(layer, b)

    accs = (acc0, acc1)
    for layer, ext in enumerate((ext0, ext1)):
        for b in range(blocks + 1):
            if b < blocks:
                if layer == 0 and b in loads:
                    loads[b].wait()
                accs[b % 2][...] = dot(adj[rows[b], :], ext[...])
            if b > 0:
                finish(layer, b - 1, accs[(b - 1) % 2][...])
        if layer == 0:
            for copy in halos[1]:
                copy.wait()
    for copy in stores:
        copy.wait()


def backward_body(core_ref, cot_hbm, w_hbm, adj_hbm, m_hbm, s_hbm, kept_ref, given_ref, cot, w, adj, m_all, s_all, turned, load_sem):
    work, width = cot.shape
    step = 512
    blocks = work // step
    parts = [pl.ds(b * step, step) for b in range(blocks)]
    pairs = [
        (s_hbm.at[1], s_all.at[1]),
        (cot_hbm, cot),
        (m_hbm.at[1], m_all.at[1]),
        (w_hbm, w),
    ]
    pairs += [(adj_hbm.at[:, parts[0]], adj.at[:, parts[0]])]
    pairs += [(s_hbm.at[0], s_all.at[0]), (m_hbm.at[0], m_all.at[0])]
    pairs += [(adj_hbm.at[:, part], adj.at[:, part]) for part in parts[1:]]
    loads = [
        pltpu.make_async_copy(here, there, load_sem.at[i]) for i, (here, there) in enumerate(pairs)
    ]
    for load in loads:
        load.start()
    for load in loads[:4]:
        load.wait()
    beta = BETAS[1]
    total = jnp.zeros((width, width), F32)
    for part in parts:
        grad_two = cot[part, :].astype(F32) * s_all[1, part, :]
        grad_two_b = grad_two.astype(BF16)
        total = total + dot_rows(m_all[1, part, :], grad_two_b)
        through = lax.dot_general(
            grad_two_b, w[1], (((1,), (1,)), ((), ())), preferred_element_type=F32
        )
        grad_mix = (1.0 - beta) * grad_two + beta * through
        turned[:, part] = jnp.transpose(grad_mix.astype(BF16))
    second = BETAS[1] * total
    total = jnp.zeros((width, width), F32)
    for b, part in enumerate(parts):
        for load in loads[4:7] if b == 0 else loads[6 + b : 7 + b]:
            load.wait()
        back = jnp.transpose(dot(turned[...], adj[:, part]))
        grad_one = (1.0 - ALPHA) * back * s_all[0, part, :]
        total = total + dot_rows(m_all[0, part, :], grad_one.astype(BF16))
    first = BETAS[0] * total
    lower = core_ref[0] == 0
    for i in range(width // 128):
        here, there = slice(128 * i, 128 * (i + 1)), pl.ds(width * i, width)
        kept_ref[there, :] = jnp.where(lower, first[:, here], second[:, here])
        given_ref[there, :] = jnp.where(lower, second[:, here], first[:, here])


def collect_body(column_ref, back_ref, out_ref):
    slots = back_ref.shape[0]
    step = 256
    lane = lax.broadcasted_iota(jnp.int32, (step, 128), 1).astype(F32)
    for b in range(out_ref.shape[0] // step):
        part = pl.ds(b * step, step)
        place = column_ref[part, :]
        hit = jnp.concatenate(
            [(place - 128.0 * c == lane).astype(F32).astype(BF16) for c in range(slots // 128)],
            axis=1,
        )
        out_ref[part, :] = dot(hit, back_ref[...]).astype(BF16)


def local(
    x_home,
    cotangent,
    owner,
    weights,
    history,
    halo_ids,
    halo_count,
    tile_rows,
    tile_cols,
    tile_count,
    tile_vals,
):
    n_wide = lax.axis_size(WIDE)
    n_hist = lax.axis_size(HIST)
    rows_here, width = x_home.shape
    work = n_wide * CAP
    halo = n_hist * HCAP
    slots = tile_vals.shape[2]

    anywhere = pl.BlockSpec(memory_space=pl.ANY)
    x = lax.axis_index("x")
    core = lax.axis_index("core")
    size = lax.axis_size("x")

    def to_owners(value):
        value = value.reshape(n_wide, CAP, width)
        return lax.all_to_all(value, WIDE, split_axis=0, concat_axis=0, tiled=True).reshape(
            work, width
        )

    send, place = pl.pallas_call(
        lambda *refs: route_body(n_wide, *refs),
        out_shape=(
            pltpu.HBM((work, width), BF16),
            jax.ShapeDtypeStruct((1, rows_here), jnp.int32),
        ),
        in_specs=vmem(1) + [anywhere],
        out_specs=(anywhere, vmem(1)[0]),
        scratch_shapes=[
            pltpu.VMEM((rows_here, width), BF16),
            pltpu.VMEM((work, width), BF16),
            pltpu.SemaphoreType.DMA,
            pltpu.SemaphoreType.DMA((work // 512,)),
        ],
        compiler_params=params(56),
        cost_estimate=cost(2 * work * rows_here * width, 2 * MIB),
        name="route",
    )(owner.reshape(1, rows_here), x_home)
    ws = to_owners(send)

    adjacency, send_cot, column = pl.pallas_call(
        prepare_body,
        out_shape=(
            pltpu.HBM((work, work + halo), BF16),
            pltpu.HBM((work, width), BF16),
            pltpu.HBM((rows_here, 128), F32),
        ),
        in_specs=smem(3) + vmem(1) + [anywhere] * 2,
        out_specs=(anywhere, anywhere, vmem(1)[0]),
        scratch_shapes=[
            pltpu.VMEM((work, work + halo), BF16),
            pltpu.VMEM((slots, TILE, TILE), BF16),
            pltpu.VMEM((rows_here, width), BF16),
            pltpu.VMEM((work, width), BF16),
            pltpu.SMEM(((work // TILE) * ((work + halo) // TILE),), jnp.int32),
            pltpu.SMEM((slots,), jnp.int32),
            pltpu.SMEM((work // TILE,), jnp.int32),
            pltpu.SMEM((slots,), jnp.int32),
            pltpu.SemaphoreType.DMA((2,)),
            pltpu.SemaphoreType.DMA((work // TILE,)),
            pltpu.SemaphoreType.DMA((work // 512,)),
        ],
        compiler_params=params(56),
        cost_estimate=cost(2 * work * rows_here * width, 20 * MIB),
        name="prepare",
    )(tile_rows[0, 0], tile_cols[0, 0], tile_count[0], place, tile_vals[0, 0], cotangent)

    live = jnp.arange(HCAP)[None, :] < halo_count[0, 0][:, None]
    wanted = jnp.where(live, halo_ids[0, 0], -1)
    wanted, place = lax.optimization_barrier((wanted, place))
    wanted = wanted.reshape(size, 2, HCAP)
    wanted = lax.dynamic_slice_in_dim(jnp.concatenate([wanted, wanted]), x, size, axis=0)

    def shift(value, by):
        return lax.ppermute(value, "x", [(i, (i + by) % size) for i in range(size)])

    asked = jnp.stack([wanted[0]] + [shift(wanted[k], k) for k in range(1, size)])
    asked_own = jnp.where(core == 0, asked[:, 0], asked[:, 1])
    asked_other = swap_cores(jnp.where(core == 0, asked[:, 1], asked[:, 0]))
    asked = jnp.stack([asked_own, asked_other]).reshape(halo, 1)
    blocks = pl.pallas_call(
        pick_body,
        out_shape=(jax.ShapeDtypeStruct((4 * HCAP, width), BF16),) * size,
        in_specs=vmem(2),
        out_specs=tuple(vmem(size)),
        compiler_params=params(12),
        cost_estimate=cost(4 * halo * history.shape[1] * width, 2 * MIB),
        name="pick",
    )(jnp.broadcast_to(asked, (halo, 128)), history)
    send_cot, ws, adjacency, blocks = lax.optimization_barrier((send_cot, ws, adjacency, blocks))
    ws_cot = to_owners(send_cot)

    pieces = [blocks[0]] + [shift(blocks[k], size - k) for k in range(1, size)]
    pieces += [swap_cores(piece) for piece in pieces]

    step = 256
    second, mixed, slopes = pl.pallas_call(
        lambda *refs: forward_body(size, *refs),
        out_shape=(
            pltpu.HBM((work, width), BF16),
            pltpu.HBM((2, work, width), BF16),
            pltpu.HBM((2, work, width), F32),
        ),
        in_specs=smem(2) + [anywhere] * (3 + 2 * size),
        out_specs=(anywhere,) * 3,
        scratch_shapes=[
            pltpu.VMEM((work, work + halo), BF16),
            pltpu.VMEM((2, width, width), BF16),
            pltpu.VMEM((work, width), BF16),
            pltpu.VMEM((work + halo, width), BF16),
            pltpu.VMEM((work + halo, width), BF16),
            pltpu.VMEM((2, work, width), BF16),
            pltpu.VMEM((2, work, width), F32),
            pltpu.VMEM((work, width), BF16),
            pltpu.VMEM((step, width), F32),
            pltpu.VMEM((step, width), F32),
            pltpu.SemaphoreType.DMA((5 + 4 * size,)),
            pltpu.SemaphoreType.DMA((2, 3, work // step)),
        ],
        compiler_params=params(56),
        cost_estimate=cost(4 * work * (work + halo + width) * width, 24 * MIB),
        name="forward",
    )(
        x.reshape(1).astype(jnp.int32),
        core.reshape(1).astype(jnp.int32),
        in_hbm(ws),
        weights,
        adjacency,
        *[in_hbm(piece) for piece in pieces],
    )
    second, ws_cot = lax.optimization_barrier((second, ws_cot))
    returned = to_owners(second)

    kept, given = pl.pallas_call(
        backward_body,
        out_shape=(jax.ShapeDtypeStruct((width * width // 128, 128), F32),) * 2,
        in_specs=smem(1) + [anywhere] * 5,
        out_specs=tuple(vmem(2)),
        scratch_shapes=[
            pltpu.VMEM((work, width), BF16),
            pltpu.VMEM((2, width, width), BF16),
            pltpu.VMEM((work, work), BF16),
            pltpu.VMEM((2, work, width), BF16),
            pltpu.VMEM((2, work, width), F32),
            pltpu.VMEM((width, work), BF16),
            pltpu.SemaphoreType.DMA((10,)),
        ],
        compiler_params=params(56),
        cost_estimate=cost(2 * work * (work + 3 * width) * width, 20 * MIB),
        name="backward",
    )(core.reshape(1).astype(jnp.int32), in_hbm(ws_cot), weights, adjacency, mixed, slopes)
    grads = reduce_rows(kept + swap_cores(given))
    grads, returned = lax.optimization_barrier((grads, returned))
    second_out = pl.pallas_call(
        collect_body,
        out_shape=jax.ShapeDtypeStruct((rows_here, width), BF16),
        in_specs=vmem(2),
        out_specs=vmem(1)[0],
        compiler_params=params(24),
        cost_estimate=cost(2 * work * rows_here * width, 2 * MIB),
        name="collect",
    )(column, returned)
    mine = sum_wide(grads, n_wide)
    mine, second_out = lax.optimization_barrier((mine, second_out))
    return (second_out, spread(mine))


def swap_cores(value):
    return lax.ppermute(value, "core", [(0, 1), (1, 0)])


def reduce_rows(kept):
    size = lax.axis_size("x")
    quarter = kept.shape[0] // size
    x = lax.axis_index("x")

    def rows_of(index):
        return lax.dynamic_slice_in_dim(kept, lax.rem(index, size) * quarter, quarter, axis=0)

    total = rows_of(x)
    for k in range(1, size):
        total = total + lax.ppermute(
            rows_of(x + k), "x", [(i, (i + k) % size) for i in range(size)]
        )
    return total


def sum_wide(part, n_wide):
    rows, lanes = part.shape
    parts = lax.all_to_all(
        part.reshape(n_wide, rows // n_wide, lanes), WIDE, split_axis=0, concat_axis=0, tiled=True
    )
    return jnp.sum(parts, axis=0, keepdims=True).astype(BF16)


def spread(mine):
    _, some, lanes = mine.shape
    every = ("x",) + WIDE
    n_every = lax.axis_size(every)
    own = lax.all_to_all(
        jnp.broadcast_to(mine, (n_every, some, lanes)),
        every,
        split_axis=0,
        concat_axis=0,
        tiled=True,
    ).reshape(n_every * some, lanes)
    other = swap_cores(own)
    core = lax.axis_index("core")
    both = [jnp.where(core == 0, own, other), jnp.where(core == 0, other, own)]
    width = math.isqrt(n_every * some * lanes)
    return jnp.stack(
        [
            jnp.concatenate([one[i : i + width] for i in range(0, n_every * some, width)], axis=1)
            for one in both
        ]
    ).astype(F32)


def solution(mesh):
    sizes = (4, mesh.shape["wide"] // 4, mesh.shape["hist"] // 2, 2)
    split = Mesh(mesh.devices.reshape(sizes), WIDE + HIST)
    rows = P(WIDE + HIST, None)
    placed = (
        rows,
        rows,
        rows,
        P(),
        P(None, HIST, None),
        P(WIDE, HIST, None, None),
        P(WIDE, HIST, None),
        P(WIDE, HIST, None),
        P(WIDE, HIST, None),
        P(WIDE, HIST),
        P(WIDE, HIST, None, None, None),
    )
    return jax.shard_map(
        local,
        mesh=split,
        in_specs=placed,
        out_specs=(rows, P()),
        check_vma=False,
    )
```

```python
import math

import jax
import jax.numpy as jnp
from jax import lax
from jax.experimental import pallas as pl
from jax.experimental.pallas import tpu as pltpu
from jax.sharding import Mesh
from jax.sharding import PartitionSpec as P

ALPHA = 0.1
BETAS = (math.log(1.5), math.log(1.25))
TILE = 128
CAP = 64
HCAP = 64
MARK = 1024.0
LIMIT = 512.0
BF16 = jnp.bfloat16
F32 = jnp.float32
MIB = 1 << 20
WIDE = ("y", "z")
HIST = ("x", "core")


def vmem(count):
    return [pl.BlockSpec(memory_space=pltpu.VMEM)] * count


def smem(count):
    return [pl.BlockSpec(memory_space=pltpu.SMEM)] * count


def params(limit):
    return pltpu.CompilerParams(vmem_limit_bytes=limit * MIB)


def cost(flops, moved):
    return pl.CostEstimate(flops=flops, bytes_accessed=moved, transcendentals=0)


def in_hbm(value):
    return pltpu.with_memory_space_constraint(value, pltpu.HBM)


def dot(a, b):
    return jnp.dot(a, b, preferred_element_type=F32)


def dot_rows(a, b):
    return lax.dot_general(a, b, (((0,), (0,)), ((), ())), preferred_element_type=F32)


def hits_of(place, start, step):
    slots = lax.broadcasted_iota(jnp.int32, (step, place.shape[1]), 0) + start
    return (slots == place).astype(F32)


def route_body(n_wide, own_ref, x_hbm, send_hbm, place_ref, x_all, send, load_sem, send_sem):
    load = pltpu.make_async_copy(x_hbm, x_all, load_sem)
    load.start()
    rows_here = own_ref.shape[1]
    blocks = rows_here // 128
    own = own_ref[...]
    hot = (own == lax.broadcasted_iota(jnp.int32, (n_wide, rows_here), 0)).astype(F32)
    hot_b = hot.astype(BF16)
    lower = lax.broadcasted_iota(jnp.int32, (128, 128), 0)
    upper = lax.broadcasted_iota(jnp.int32, (128, 128), 1)
    earlier = (lower < upper).astype(F32).astype(BF16)
    parts = [slice(128 * b, 128 * (b + 1)) for b in range(blocks)]
    inside = dot(jnp.concatenate([hot_b[:, part] for part in parts], axis=0), earlier)
    before = jnp.zeros((n_wide, 1), F32)
    ranks = []
    for b, part in enumerate(parts):
        seen = inside[n_wide * b : n_wide * (b + 1)] + before
        ranks.append(jnp.sum(seen * hot[:, part], axis=0, keepdims=True))
        before = before + jnp.sum(hot[:, part], axis=1, keepdims=True)
    rank = jnp.concatenate(ranks, axis=1)
    place_ref[...] = own * CAP + rank.astype(jnp.int32)
    by_rank = (rank == lax.broadcasted_iota(jnp.int32, (CAP, rows_here), 0).astype(F32)).astype(F32)
    by_rank = by_rank.astype(BF16)
    slot = lax.broadcasted_iota(jnp.int32, (CAP, 1), 0).astype(F32)
    load.wait()
    peers = 8
    step = peers * CAP
    stores = []
    for c in range(n_wide // peers):
        part = pl.ds(c * step, step)
        group = range(c * peers, (c + 1) * peers)
        hit = jnp.concatenate([by_rank * hot_b[o : o + 1, :] for o in group], axis=0)
        held = jnp.concatenate([slot < before[o : o + 1, :] for o in group], axis=0)
        send[part, :] = jnp.where(held, dot(hit, x_all[...]), MARK).astype(BF16)
        store = pltpu.make_async_copy(send.at[part], send_hbm.at[part], send_sem.at[c])
        store.start()
        stores.append(store)
    for store in stores:
        store.wait()


def prepare_body(
    rows_ref, cols_ref, count_ref, place_ref, vals_hbm, cot_hbm, adj_hbm, send_hbm, column_ref,
    adj, vals, cot, send, head, following, row_head, row_next, load_sem, adj_sem, send_sem,
):
    loads = (
        pltpu.make_async_copy(vals_hbm, vals, load_sem.at[0]),
        pltpu.make_async_copy(cot_hbm, cot, load_sem.at[1]),
    )
    for load in loads:
        load.start()
    count = count_ref[0]
    n_rows, wide = adj.shape[0] // TILE, adj.shape[1] // TILE
    for r in range(n_rows):
        row_head[r] = -1

    def clear(k, carry):
        head[rows_ref[k] * wide + cols_ref[k]] = -1
        return carry

    lax.fori_loop(0, count, clear, 0)

    def chain(i, carry):
        k = count - 1 - i
        row = rows_ref[k]
        cell = row * wide + cols_ref[k]
        following[k] = head[cell]
        head[cell] = k
        row_next[k] = row_head[row]
        row_head[row] = k
        return carry

    lax.fori_loop(0, count, chain, 0)
    loads[0].wait()

    def row_copy(r):
        part = pl.ds(pl.multiple_of(r * TILE, TILE), TILE)
        return pltpu.make_async_copy(adj.at[part], adj_hbm.at[part], adj_sem.at[r])

    def fill(r, carry):
        part = pl.ds(pl.multiple_of(r * TILE, TILE), TILE)
        adj[part, :] = jnp.zeros((TILE, adj.shape[1]), BF16)

        def place_tile(k):
            col = cols_ref[k]

            @pl.when(head[r * wide + col] == k)
            def _():
                def more(state):
                    at, total = state
                    return following[at], total + vals[at].astype(F32)

                _, total = lax.while_loop(
                    lambda state: state[0] >= 0, more, (following[k], vals[k].astype(F32))
                )
                adj[part, pl.ds(pl.multiple_of(col * TILE, TILE), TILE)] = total.astype(BF16)

            return row_next[k]

        lax.while_loop(lambda k: k >= 0, place_tile, row_head[r])
        row_copy(r).start()
        return carry

    lax.fori_loop(0, n_rows, fill, 0)
    loads[1].wait()
    place = place_ref[...]
    step = 512
    stores = []
    for c in range(send.shape[0] // step):
        part = pl.ds(c * step, step)
        hit = hits_of(place, c * step, step).astype(BF16)
        send[part, :] = dot(hit, cot[...]).astype(BF16)
        store = pltpu.make_async_copy(send.at[part], send_hbm.at[part], send_sem.at[c])
        store.start()
        stores.append(store)
    for b in range(place.shape[1] // 128):
        part = place[:, 128 * b : 128 * (b + 1)].astype(F32)
        column_ref[pl.ds(128 * b, 128), :] = jnp.transpose(jnp.broadcast_to(part, (128, 128)))
    for store in stores:
        store.wait()

    def drain(r, carry):
        row_copy(r).wait()
        return carry

    lax.fori_loop(0, n_rows, drain, 0)


def pick_body(ids_ref, history_ref, *block_refs):
    slots = ids_ref.shape[0]
    here = history_ref.shape[1]
    lane = lax.broadcasted_iota(jnp.int32, (slots, 128), 1)
    ids = ids_ref[...]
    hit = jnp.concatenate(
        [(ids - 128 * c == lane).astype(F32).astype(BF16) for c in range(here // 128)], axis=1
    )
    size = len(block_refs)
    for layer in range(2):
        rows = dot(hit, history_ref[layer]).astype(BF16)
        for side in range(2):
            for k, ref in enumerate(block_refs):
                at = (side * size + k) * HCAP
                ref[pl.ds((2 * side + layer) * HCAP, HCAP), :] = rows[at : at + HCAP]


def forward_body(size, x_ref, core_ref, ws_hbm, w_hbm, adj_hbm, *rest):
    pieces = rest[:size], rest[size : 2 * size]
    out_hbm, m_hbm, s_hbm, adj, w, ws, ext0, ext1, m_all, s_all, out, acc0, acc1, load_sem, keep_sem = rest[2 * size :]
    work, width = ws.shape
    step = acc0.shape[0]
    blocks = work // step
    rows = [pl.ds(b * step, step) for b in range(blocks)]
    x, core = x_ref[0], core_ref[0]
    first = pltpu.make_async_copy(ws_hbm, ws, load_sem.at[0])
    first.start()
    loads = {}

    def load_rows(b, until):
        part = pl.ds(b * step, (until - b) * step)
        sem = load_sem.at[2 + 4 * size + len(loads)]
        loads[b] = pltpu.make_async_copy(adj_hbm.at[part], adj.at[part], sem)
        loads[b].start()

    def load_halo(layer, ext):
        copies = []
        for k in range(size):
            for side in range(2):
                shard = lax.rem(x + k, size) * 2 + lax.rem(core + side, 2)
                there = pl.ds(pl.multiple_of(work + shard * HCAP, HCAP), HCAP)
                here = pl.ds((2 * side + layer) * HCAP, HCAP)
                sem = load_sem.at[2 + (layer * size + k) * 2 + side]
                copies.append(pltpu.make_async_copy(pieces[side][k].at[here], ext.at[there], sem))
                copies[-1].start()
        return copies

    load_rows(0, 1)
    halos = [load_halo(0, ext0)]
    load_rows(1, 4)
    weight = pltpu.make_async_copy(w_hbm, w, load_sem.at[1])
    weight.start()
    load_rows(4, blocks)
    halos.append(load_halo(1, ext1))
    first.wait()
    for part in rows:
        got = ws[part, :].astype(F32)
        ext0[part, :] = jnp.where(got < LIMIT, got, 0.0).astype(BF16)
    for copy in halos[0]:
        copy.wait()
    weight.wait()
    stores = []

    def store(here, there, *at):
        copy = pltpu.make_async_copy(here, there, keep_sem.at[*at])
        copy.start()
        stores.append(copy)

    def keep(layer, b):
        part = rows[b]
        store(m_all.at[layer, part], m_hbm.at[layer, part], layer, 0, b)
        store(s_all.at[layer, part], s_hbm.at[layer, part], layer, 1, b)

    def finish(layer, b, support):
        part = rows[b]
        beta = BETAS[layer]
        mixed = (1.0 - ALPHA) * support + ALPHA * ext0[part, :].astype(F32)
        mixed_b = mixed.astype(BF16)
        m_all[layer, part, :] = mixed_b
        pre = (1.0 - beta) * mixed + beta * dot(mixed_b, w[layer])
        sig = jax.nn.sigmoid(pre)
        valid = ws[part, :].astype(F32) < LIMIT
        raw = pre * sig
        new = jnp.where(valid, raw, 0.0).astype(BF16)
        s_all[layer, part, :] = jnp.where(valid, sig + raw * (1.0 - sig), 0.0)
        (ext1, out)[layer][part, :] = new
        if layer == 1:
            store(out.at[part], out_hbm.at[part], 1, 2, b)
        keep(layer, b)

    accs = (acc0, acc1)
    for layer, ext in enumerate((ext0, ext1)):
        for b in range(blocks + 1):
            if b < blocks:
                if layer == 0 and b in loads:
                    loads[b].wait()
                accs[b % 2][...] = dot(adj[rows[b], :], ext[...])
            if b > 0:
                finish(layer, b - 1, accs[(b - 1) % 2][...])
        if layer == 0:
            for copy in halos[1]:
                copy.wait()
    for copy in stores:
        copy.wait()


def backward_body(core_ref, cot_hbm, w_hbm, adj_hbm, m_hbm, s_hbm, kept_ref, given_ref, cot, w, adj, m_all, s_all, turned, load_sem):
    work, width = cot.shape
    step = 512
    blocks = work // step
    parts = [pl.ds(b * step, step) for b in range(blocks)]
    pairs = [
        (s_hbm.at[1], s_all.at[1]),
        (cot_hbm, cot),
        (m_hbm.at[1], m_all.at[1]),
        (w_hbm, w),
    ]
    pairs += [(adj_hbm.at[:, parts[0]], adj.at[:, parts[0]])]
    pairs += [(s_hbm.at[0], s_all.at[0]), (m_hbm.at[0], m_all.at[0])]
    pairs += [(adj_hbm.at[:, part], adj.at[:, part]) for part in parts[1:]]
    loads = [
        pltpu.make_async_copy(here, there, load_sem.at[i]) for i, (here, there) in enumerate(pairs)
    ]
    for load in loads:
        load.start()
    for load in loads[:4]:
        load.wait()
    beta = BETAS[1]
    total = jnp.zeros((width, width), F32)
    for part in parts:
        grad_two = cot[part, :].astype(F32) * s_all[1, part, :]
        grad_two_b = grad_two.astype(BF16)
        total = total + dot_rows(m_all[1, part, :], grad_two_b)
        through = lax.dot_general(
            grad_two_b, w[1], (((1,), (1,)), ((), ())), preferred_element_type=F32
        )
        grad_mix = (1.0 - beta) * grad_two + beta * through
        turned[:, part] = jnp.transpose(grad_mix.astype(BF16))
    second = BETAS[1] * total
    total = jnp.zeros((width, width), F32)
    for b, part in enumerate(parts):
        for load in loads[4:7] if b == 0 else loads[6 + b : 7 + b]:
            load.wait()
        back = jnp.transpose(dot(turned[...], adj[:, part]))
        grad_one = (1.0 - ALPHA) * back * s_all[0, part, :]
        total = total + dot_rows(m_all[0, part, :], grad_one.astype(BF16))
    first = BETAS[0] * total
    lower = core_ref[0] == 0
    for i in range(width // 128):
        here, there = slice(128 * i, 128 * (i + 1)), pl.ds(width * i, width)
        kept_ref[there, :] = jnp.where(lower, first[:, here], second[:, here])
        given_ref[there, :] = jnp.where(lower, second[:, here], first[:, here])


def collect_body(column_ref, back_ref, out_ref):
    slots = back_ref.shape[0]
    step = 256
    lane = lax.broadcasted_iota(jnp.int32, (step, 128), 1).astype(F32)
    for b in range(out_ref.shape[0] // step):
        part = pl.ds(b * step, step)
        place = column_ref[part, :]
        hit = jnp.concatenate(
            [(place - 128.0 * c == lane).astype(F32).astype(BF16) for c in range(slots // 128)],
            axis=1,
        )
        out_ref[part, :] = dot(hit, back_ref[...]).astype(BF16)


def local(
    x_home,
    cotangent,
    owner,
    weights,
    history,
    halo_ids,
    halo_count,
    tile_rows,
    tile_cols,
    tile_count,
    tile_vals,
):
    n_wide = lax.axis_size(WIDE)
    n_hist = lax.axis_size(HIST)
    rows_here, width = x_home.shape
    work = n_wide * CAP
    halo = n_hist * HCAP
    slots = tile_vals.shape[2]

    anywhere = pl.BlockSpec(memory_space=pl.ANY)
    x = lax.axis_index("x")
    core = lax.axis_index("core")
    size = lax.axis_size("x")

    def to_owners(value):
        value = value.reshape(n_wide, CAP, width)
        return lax.all_to_all(value, WIDE, split_axis=0, concat_axis=0, tiled=True).reshape(
            work, width
        )

    send, place = pl.pallas_call(
        lambda *refs: route_body(n_wide, *refs),
        out_shape=(
            pltpu.HBM((work, width), BF16),
            jax.ShapeDtypeStruct((1, rows_here), jnp.int32),
        ),
        in_specs=vmem(1) + [anywhere],
        out_specs=(anywhere, vmem(1)[0]),
        scratch_shapes=[
            pltpu.VMEM((rows_here, width), BF16),
            pltpu.VMEM((work, width), BF16),
            pltpu.SemaphoreType.DMA,
            pltpu.SemaphoreType.DMA((work // 512,)),
        ],
        compiler_params=params(56),
        cost_estimate=cost(2 * work * rows_here * width, 2 * MIB),
        name="route",
    )(owner.reshape(1, rows_here), x_home)
    ws = to_owners(send)

    adjacency, send_cot, column = pl.pallas_call(
        prepare_body,
        out_shape=(
            pltpu.HBM((work, work + halo), BF16),
            pltpu.HBM((work, width), BF16),
            pltpu.HBM((rows_here, 128), F32),
        ),
        in_specs=smem(3) + vmem(1) + [anywhere] * 2,
        out_specs=(anywhere, anywhere, vmem(1)[0]),
        scratch_shapes=[
            pltpu.VMEM((work, work + halo), BF16),
            pltpu.VMEM((slots, TILE, TILE), BF16),
            pltpu.VMEM((rows_here, width), BF16),
            pltpu.VMEM((work, width), BF16),
            pltpu.SMEM(((work // TILE) * ((work + halo) // TILE),), jnp.int32),
            pltpu.SMEM((slots,), jnp.int32),
            pltpu.SMEM((work // TILE,), jnp.int32),
            pltpu.SMEM((slots,), jnp.int32),
            pltpu.SemaphoreType.DMA((2,)),
            pltpu.SemaphoreType.DMA((work // TILE,)),
            pltpu.SemaphoreType.DMA((work // 512,)),
        ],
        compiler_params=params(56),
        cost_estimate=cost(2 * work * rows_here * width, 20 * MIB),
        name="prepare",
    )(tile_rows[0, 0], tile_cols[0, 0], tile_count[0], place, tile_vals[0, 0], cotangent)

    live = jnp.arange(HCAP)[None, :] < halo_count[0, 0][:, None]
    wanted = jnp.where(live, halo_ids[0, 0], -1)
    wanted, place = lax.optimization_barrier((wanted, place))
    wanted = wanted.reshape(size, 2, HCAP)
    wanted = lax.dynamic_slice_in_dim(jnp.concatenate([wanted, wanted]), x, size, axis=0)

    def shift(value, by):
        return lax.ppermute(value, "x", [(i, (i + by) % size) for i in range(size)])

    asked = jnp.stack([wanted[0]] + [shift(wanted[k], k) for k in range(1, size)])
    asked_own = jnp.where(core == 0, asked[:, 0], asked[:, 1])
    asked_other = swap_cores(jnp.where(core == 0, asked[:, 1], asked[:, 0]))
    asked = jnp.stack([asked_own, asked_other]).reshape(halo, 1)
    blocks = pl.pallas_call(
        pick_body,
        out_shape=(jax.ShapeDtypeStruct((4 * HCAP, width), BF16),) * size,
        in_specs=vmem(2),
        out_specs=tuple(vmem(size)),
        compiler_params=params(12),
        cost_estimate=cost(4 * halo * history.shape[1] * width, 2 * MIB),
        name="pick",
    )(jnp.broadcast_to(asked, (halo, 128)), history)
    send_cot, ws, adjacency, blocks = lax.optimization_barrier((send_cot, ws, adjacency, blocks))
    ws_cot = to_owners(send_cot)

    pieces = [blocks[0]] + [shift(blocks[k], size - k) for k in range(1, size)]
    pieces += [swap_cores(piece) for piece in pieces]

    step = 256
    second, mixed, slopes = pl.pallas_call(
        lambda *refs: forward_body(size, *refs),
        out_shape=(
            pltpu.HBM((work, width), BF16),
            pltpu.HBM((2, work, width), BF16),
            pltpu.HBM((2, work, width), F32),
        ),
        in_specs=smem(2) + [anywhere] * (3 + 2 * size),
        out_specs=(anywhere,) * 3,
        scratch_shapes=[
            pltpu.VMEM((work, work + halo), BF16),
            pltpu.VMEM((2, width, width), BF16),
            pltpu.VMEM((work, width), BF16),
            pltpu.VMEM((work + halo, width), BF16),
            pltpu.VMEM((work + halo, width), BF16),
            pltpu.VMEM((2, work, width), BF16),
            pltpu.VMEM((2, work, width), F32),
            pltpu.VMEM((work, width), BF16),
            pltpu.VMEM((step, width), F32),
            pltpu.VMEM((step, width), F32),
            pltpu.SemaphoreType.DMA((5 + 4 * size,)),
            pltpu.SemaphoreType.DMA((2, 3, work // step)),
        ],
        compiler_params=params(56),
        cost_estimate=cost(4 * work * (work + halo + width) * width, 24 * MIB),
        name="forward",
    )(
        x.reshape(1).astype(jnp.int32),
        core.reshape(1).astype(jnp.int32),
        in_hbm(ws),
        weights,
        adjacency,
        *[in_hbm(piece) for piece in pieces],
    )
    second, ws_cot = lax.optimization_barrier((second, ws_cot))
    returned = to_owners(second)

    kept, given = pl.pallas_call(
        backward_body,
        out_shape=(jax.ShapeDtypeStruct((width * width // 128, 128), F32),) * 2,
        in_specs=smem(1) + [anywhere] * 5,
        out_specs=tuple(vmem(2)),
        scratch_shapes=[
            pltpu.VMEM((work, width), BF16),
            pltpu.VMEM((2, width, width), BF16),
            pltpu.VMEM((work, work), BF16),
            pltpu.VMEM((2, work, width), BF16),
            pltpu.VMEM((2, work, width), F32),
            pltpu.VMEM((width, work), BF16),
            pltpu.SemaphoreType.DMA((10,)),
        ],
        compiler_params=params(56),
        cost_estimate=cost(2 * work * (work + 3 * width) * width, 20 * MIB),
        name="backward",
    )(core.reshape(1).astype(jnp.int32), in_hbm(ws_cot), weights, adjacency, mixed, slopes)
    grads = reduce_rows(reduce_rows(kept + swap_cores(given), "x"), "y")
    grads, returned = lax.optimization_barrier((grads, returned))
    second_out = pl.pallas_call(
        collect_body,
        out_shape=jax.ShapeDtypeStruct((rows_here, width), BF16),
        in_specs=vmem(2),
        out_specs=vmem(1)[0],
        compiler_params=params(24),
        cost_estimate=cost(2 * work * rows_here * width, 2 * MIB),
        name="collect",
    )(column, returned)
    mine = jnp.sum(from_all(grads, "z"), axis=0).astype(BF16)
    mine, second_out = lax.optimization_barrier((mine, second_out))
    return (second_out, spread(mine))


def swap_cores(value):
    return lax.ppermute(value, "core", [(0, 1), (1, 0)])


def reduce_rows(kept, axis):
    size = lax.axis_size(axis)
    share = kept.shape[0] // size
    here = lax.axis_index(axis)

    def rows_of(index):
        return lax.dynamic_slice_in_dim(kept, lax.rem(index, size) * share, share, axis=0)

    total = rows_of(here)
    for k in range(1, size):
        total = total + lax.ppermute(
            rows_of(here + k), axis, [(i, (i + k) % size) for i in range(size)]
        )
    return total


def from_all(value, axes):
    value = jnp.broadcast_to(value[None], (lax.axis_size(axes),) + value.shape)
    return lax.all_to_all(value, axes, split_axis=0, concat_axis=0, tiled=True)


def spread(mine):
    parts = from_all(mine, ("x", "y"))
    own = parts.reshape(-1, parts.shape[-1])
    other = swap_cores(own)
    core = lax.axis_index("core")
    both = [jnp.where(core == 0, own, other), jnp.where(core == 0, other, own)]
    rows, lanes = own.shape
    width = math.isqrt(rows * lanes)
    return jnp.stack(
        [
            jnp.concatenate([one[i : i + width] for i in range(0, rows, width)], axis=1)
            for one in both
        ]
    ).astype(F32)


def solution(mesh):
    sizes = (4, mesh.shape["wide"] // 4, mesh.shape["hist"] // 2, 2)
    split = Mesh(mesh.devices.reshape(sizes), WIDE + HIST)
    rows = P(WIDE + HIST, None)
    placed = (
        rows,
        rows,
        rows,
        P(),
        P(None, HIST, None),
        P(WIDE, HIST, None, None),
        P(WIDE, HIST, None),
        P(WIDE, HIST, None),
        P(WIDE, HIST, None),
        P(WIDE, HIST),
        P(WIDE, HIST, None, None, None),
    )
    return jax.shard_map(
        local,
        mesh=split,
        in_specs=placed,
        out_specs=(rows, P()),
        check_vma=False,
    )
```

```python
import math

import jax
import jax.numpy as jnp
from jax import lax
from jax.experimental import pallas as pl
from jax.experimental.pallas import tpu as pltpu
from jax.sharding import Mesh
from jax.sharding import PartitionSpec as P

ALPHA = 0.1
BETAS = (math.log(1.5), math.log(1.25))
TILE = 128
CAP = 64
HCAP = 64
MARK = 1024.0
LIMIT = 512.0
BF16 = jnp.bfloat16
F32 = jnp.float32
MIB = 1 << 20
WIDE = ("y", "z")
HIST = ("x", "core")


def vmem(count):
    return [pl.BlockSpec(memory_space=pltpu.VMEM)] * count


def smem(count):
    return [pl.BlockSpec(memory_space=pltpu.SMEM)] * count


def params(limit):
    return pltpu.CompilerParams(vmem_limit_bytes=limit * MIB)


def cost(flops, moved):
    return pl.CostEstimate(flops=flops, bytes_accessed=moved, transcendentals=0)


def in_hbm(value):
    return pltpu.with_memory_space_constraint(value, pltpu.HBM)


def dot(a, b):
    return jnp.dot(a, b, preferred_element_type=F32)


def dot_rows(a, b):
    return lax.dot_general(a, b, (((0,), (0,)), ((), ())), preferred_element_type=F32)


def hits_of(place, start, step):
    slots = lax.broadcasted_iota(jnp.int32, (step, place.shape[1]), 0) + start
    return (slots == place).astype(F32)


def route_body(n_wide, own_hbm, x_hbm, send_hbm, place_hbm, own_all, place_all, x_all, send, load_sem, send_sem):
    first = pltpu.make_async_copy(own_hbm, own_all, load_sem.at[0])
    first.start()
    load = pltpu.make_async_copy(x_hbm, x_all, load_sem.at[1])
    load.start()
    rows_here = own_all.shape[1]
    blocks = rows_here // 128
    first.wait()
    own = own_all[...]
    hot = (own == lax.broadcasted_iota(jnp.int32, (n_wide, rows_here), 0)).astype(F32)
    hot_b = hot.astype(BF16)
    lower = lax.broadcasted_iota(jnp.int32, (128, 128), 0)
    upper = lax.broadcasted_iota(jnp.int32, (128, 128), 1)
    earlier = (lower < upper).astype(F32).astype(BF16)
    parts = [slice(128 * b, 128 * (b + 1)) for b in range(blocks)]
    inside = dot(jnp.concatenate([hot_b[:, part] for part in parts], axis=0), earlier)
    before = jnp.zeros((n_wide, 1), F32)
    ranks = []
    for b, part in enumerate(parts):
        seen = inside[n_wide * b : n_wide * (b + 1)] + before
        ranks.append(jnp.sum(seen * hot[:, part], axis=0, keepdims=True))
        before = before + jnp.sum(hot[:, part], axis=1, keepdims=True)
    rank = jnp.concatenate(ranks, axis=1)
    place_all[...] = own * CAP + rank.astype(jnp.int32)
    stores = [pltpu.make_async_copy(place_all, place_hbm, load_sem.at[2])]
    stores[0].start()
    by_rank = (rank == lax.broadcasted_iota(jnp.int32, (CAP, rows_here), 0).astype(F32)).astype(F32)
    by_rank = by_rank.astype(BF16)
    slot = lax.broadcasted_iota(jnp.int32, (CAP, 1), 0).astype(F32)
    load.wait()
    peers = 8
    step = peers * CAP
    for c in range(n_wide // peers):
        part = pl.ds(c * step, step)
        group = range(c * peers, (c + 1) * peers)
        hit = jnp.concatenate([by_rank * hot_b[o : o + 1, :] for o in group], axis=0)
        held = jnp.concatenate([slot < before[o : o + 1, :] for o in group], axis=0)
        send[part, :] = jnp.where(held, dot(hit, x_all[...]), MARK).astype(BF16)
        store = pltpu.make_async_copy(send.at[part], send_hbm.at[part], send_sem.at[c])
        store.start()
        stores.append(store)
    for store in stores:
        store.wait()


def prepare_body(
    rows_ref, cols_ref, count_ref, place_ref, vals, cot_hbm, adj_hbm, send_hbm, column_ref,
    adj, cot, send, head, following, row_head, row_next, load_sem, adj_sem, send_sem,
):
    load = pltpu.make_async_copy(cot_hbm, cot, load_sem)
    load.start()
    count = count_ref[0]
    n_rows, wide = adj.shape[0] // TILE, adj.shape[1] // TILE
    for r in range(n_rows):
        row_head[r] = -1

    def clear(k, carry):
        head[rows_ref[k] * wide + cols_ref[k]] = -1
        return carry

    lax.fori_loop(0, count, clear, 0)

    def chain(i, carry):
        k = count - 1 - i
        row = rows_ref[k]
        cell = row * wide + cols_ref[k]
        following[k] = head[cell]
        head[cell] = k
        row_next[k] = row_head[row]
        row_head[row] = k
        return carry

    lax.fori_loop(0, count, chain, 0)

    def row_copy(r):
        part = pl.ds(pl.multiple_of(r * TILE, TILE), TILE)
        return pltpu.make_async_copy(adj.at[part], adj_hbm.at[part], adj_sem.at[r])

    def fill(r, carry):
        part = pl.ds(pl.multiple_of(r * TILE, TILE), TILE)
        adj[part, :] = jnp.zeros((TILE, adj.shape[1]), BF16)

        def place_tile(k):
            col = cols_ref[k]

            @pl.when(head[r * wide + col] == k)
            def _():
                def more(state):
                    at, total = state
                    return following[at], total + vals[at].astype(F32)

                _, total = lax.while_loop(
                    lambda state: state[0] >= 0, more, (following[k], vals[k].astype(F32))
                )
                adj[part, pl.ds(pl.multiple_of(col * TILE, TILE), TILE)] = total.astype(BF16)

            return row_next[k]

        lax.while_loop(lambda k: k >= 0, place_tile, row_head[r])
        row_copy(r).start()
        return carry

    lax.fori_loop(0, n_rows, fill, 0)
    load.wait()
    place = place_ref[...]
    step = 512
    stores = []
    for c in range(send.shape[0] // step):
        part = pl.ds(c * step, step)
        hit = hits_of(place, c * step, step).astype(BF16)
        send[part, :] = dot(hit, cot[...]).astype(BF16)
        store = pltpu.make_async_copy(send.at[part], send_hbm.at[part], send_sem.at[c])
        store.start()
        stores.append(store)
    for b in range(place.shape[1] // 128):
        part = place[:, 128 * b : 128 * (b + 1)].astype(F32)
        column_ref[pl.ds(128 * b, 128), :] = jnp.transpose(jnp.broadcast_to(part, (128, 128)))
    for store in stores:
        store.wait()

    def drain(r, carry):
        row_copy(r).wait()
        return carry

    lax.fori_loop(0, n_rows, drain, 0)


def pick_body(ids_ref, history_ref, *block_refs):
    slots = ids_ref.shape[0]
    here = history_ref.shape[1]
    lane = lax.broadcasted_iota(jnp.int32, (slots, 128), 1)
    ids = ids_ref[...]
    hit = jnp.concatenate(
        [(ids - 128 * c == lane).astype(F32).astype(BF16) for c in range(here // 128)], axis=1
    )
    size = len(block_refs)
    for layer in range(2):
        rows = dot(hit, history_ref[layer]).astype(BF16)
        for side in range(2):
            for k, ref in enumerate(block_refs):
                at = (side * size + k) * HCAP
                ref[pl.ds((2 * side + layer) * HCAP, HCAP), :] = rows[at : at + HCAP]


def forward_body(size, x_ref, core_ref, ws_hbm, w_hbm, adj_hbm, *rest):
    pieces = rest[:size], rest[size : 2 * size]
    out_hbm, m_hbm, s_hbm, adj, w, ws, ext0, ext1, m_all, s_all, out, acc0, acc1, load_sem, keep_sem = rest[2 * size :]
    work, width = ws.shape
    step = acc0.shape[0]
    blocks = work // step
    rows = [pl.ds(b * step, step) for b in range(blocks)]
    x, core = x_ref[0], core_ref[0]
    first = pltpu.make_async_copy(ws_hbm, ws, load_sem.at[0])
    first.start()
    loads = {}

    def load_rows(b, until):
        part = pl.ds(b * step, (until - b) * step)
        sem = load_sem.at[2 + 4 * size + len(loads)]
        loads[b] = pltpu.make_async_copy(adj_hbm.at[part], adj.at[part], sem)
        loads[b].start()

    def load_halo(layer, ext):
        copies = []
        for k in range(size):
            for side in range(2):
                shard = lax.rem(x + k, size) * 2 + lax.rem(core + side, 2)
                there = pl.ds(pl.multiple_of(work + shard * HCAP, HCAP), HCAP)
                here = pl.ds((2 * side + layer) * HCAP, HCAP)
                sem = load_sem.at[2 + (layer * size + k) * 2 + side]
                copies.append(pltpu.make_async_copy(pieces[side][k].at[here], ext.at[there], sem))
                copies[-1].start()
        return copies

    load_rows(0, 1)
    halos = [load_halo(0, ext0)]
    load_rows(1, 4)
    weight = pltpu.make_async_copy(w_hbm, w, load_sem.at[1])
    weight.start()
    load_rows(4, blocks)
    halos.append(load_halo(1, ext1))
    first.wait()
    for part in rows:
        got = ws[part, :].astype(F32)
        ext0[part, :] = jnp.where(got < LIMIT, got, 0.0).astype(BF16)
    for copy in halos[0]:
        copy.wait()
    weight.wait()
    stores = []

    def store(here, there, *at):
        copy = pltpu.make_async_copy(here, there, keep_sem.at[*at])
        copy.start()
        stores.append(copy)

    def keep(layer, b):
        part = rows[b]
        store(m_all.at[layer, part], m_hbm.at[layer, part], layer, 0, b)
        store(s_all.at[layer, part], s_hbm.at[layer, part], layer, 1, b)

    def finish(layer, b, support):
        part = rows[b]
        beta = BETAS[layer]
        mixed = (1.0 - ALPHA) * support + ALPHA * ext0[part, :].astype(F32)
        mixed_b = mixed.astype(BF16)
        m_all[layer, part, :] = mixed_b
        pre = (1.0 - beta) * mixed + beta * dot(mixed_b, w[layer])
        sig = jax.nn.sigmoid(pre)
        valid = ws[part, :].astype(F32) < LIMIT
        raw = pre * sig
        new = jnp.where(valid, raw, 0.0).astype(BF16)
        s_all[layer, part, :] = jnp.where(valid, sig + raw * (1.0 - sig), 0.0)
        (ext1, out)[layer][part, :] = new
        if layer == 1:
            store(out.at[part], out_hbm.at[part], 1, 2, b)
        keep(layer, b)

    accs = (acc0, acc1)
    for layer, ext in enumerate((ext0, ext1)):
        for b in range(blocks + 1):
            if b < blocks:
                if layer == 0 and b in loads:
                    loads[b].wait()
                accs[b % 2][...] = dot(adj[rows[b], :], ext[...])
            if b > 0:
                finish(layer, b - 1, accs[(b - 1) % 2][...])
        if layer == 0:
            for copy in halos[1]:
                copy.wait()
    for copy in stores:
        copy.wait()


def backward_body(core_ref, cot_hbm, w_hbm, adj_hbm, m_hbm, s_hbm, kept_ref, given_ref, cot, w, adj, m_all, s_all, turned, load_sem):
    work, width = cot.shape
    step = 512
    blocks = work // step
    parts = [pl.ds(b * step, step) for b in range(blocks)]
    pairs = [
        (s_hbm.at[1], s_all.at[1]),
        (cot_hbm, cot),
        (m_hbm.at[1], m_all.at[1]),
        (w_hbm, w),
    ]
    pairs += [(adj_hbm.at[:, parts[0]], adj.at[:, parts[0]])]
    pairs += [(s_hbm.at[0], s_all.at[0]), (m_hbm.at[0], m_all.at[0])]
    pairs += [(adj_hbm.at[:, part], adj.at[:, part]) for part in parts[1:]]
    loads = [
        pltpu.make_async_copy(here, there, load_sem.at[i]) for i, (here, there) in enumerate(pairs)
    ]
    for load in loads:
        load.start()
    for load in loads[:4]:
        load.wait()
    beta = BETAS[1]
    total = jnp.zeros((width, width), F32)
    for part in parts:
        grad_two = cot[part, :].astype(F32) * s_all[1, part, :]
        grad_two_b = grad_two.astype(BF16)
        total = total + dot_rows(m_all[1, part, :], grad_two_b)
        through = lax.dot_general(
            grad_two_b, w[1], (((1,), (1,)), ((), ())), preferred_element_type=F32
        )
        grad_mix = (1.0 - beta) * grad_two + beta * through
        turned[:, part] = jnp.transpose(grad_mix.astype(BF16))
    second = BETAS[1] * total
    total = jnp.zeros((width, width), F32)
    for b, part in enumerate(parts):
        for load in loads[4:7] if b == 0 else loads[6 + b : 7 + b]:
            load.wait()
        back = jnp.transpose(dot(turned[...], adj[:, part]))
        grad_one = (1.0 - ALPHA) * back * s_all[0, part, :]
        total = total + dot_rows(m_all[0, part, :], grad_one.astype(BF16))
    first = BETAS[0] * total
    lower = core_ref[0] == 0
    for i in range(width // 128):
        here, there = slice(128 * i, 128 * (i + 1)), pl.ds(width * i, width)
        kept_ref[there, :] = jnp.where(lower, first[:, here], second[:, here])
        given_ref[there, :] = jnp.where(lower, second[:, here], first[:, here])


def collect_body(column_ref, back_ref, out_ref):
    slots = back_ref.shape[0]
    step = 256
    lane = lax.broadcasted_iota(jnp.int32, (step, 128), 1).astype(F32)
    for b in range(out_ref.shape[0] // step):
        part = pl.ds(b * step, step)
        place = column_ref[part, :]
        hit = jnp.concatenate(
            [(place - 128.0 * c == lane).astype(F32).astype(BF16) for c in range(slots // 128)],
            axis=1,
        )
        out_ref[part, :] = dot(hit, back_ref[...]).astype(BF16)


def local(
    x_home,
    cotangent,
    owner,
    weights,
    history,
    halo_ids,
    halo_count,
    tile_rows,
    tile_cols,
    tile_count,
    tile_vals,
):
    n_wide = lax.axis_size(WIDE)
    n_hist = lax.axis_size(HIST)
    rows_here, width = x_home.shape
    work = n_wide * CAP
    halo = n_hist * HCAP
    slots = tile_vals.shape[2]

    anywhere = pl.BlockSpec(memory_space=pl.ANY)
    x = lax.axis_index("x")
    core = lax.axis_index("core")
    size = lax.axis_size("x")

    def to_owners(value):
        value = value.reshape(n_wide, CAP, width)
        return lax.all_to_all(value, WIDE, split_axis=0, concat_axis=0, tiled=True).reshape(
            work, width
        )

    send, place = pl.pallas_call(
        lambda *refs: route_body(n_wide, *refs),
        out_shape=(
            pltpu.HBM((work, width), BF16),
            pltpu.HBM((1, rows_here), jnp.int32),
        ),
        in_specs=[anywhere] * 2,
        out_specs=(anywhere,) * 2,
        scratch_shapes=[
            pltpu.VMEM((1, rows_here), jnp.int32),
            pltpu.VMEM((1, rows_here), jnp.int32),
            pltpu.VMEM((rows_here, width), BF16),
            pltpu.VMEM((work, width), BF16),
            pltpu.SemaphoreType.DMA((3,)),
            pltpu.SemaphoreType.DMA((work // 512,)),
        ],
        compiler_params=params(56),
        cost_estimate=cost(2 * work * rows_here * width, 2 * MIB),
        name="route",
    )(owner.reshape(1, rows_here), x_home)
    ws = to_owners(send)

    adjacency, send_cot, column = pl.pallas_call(
        prepare_body,
        out_shape=(
            pltpu.HBM((work, work + halo), BF16),
            pltpu.HBM((work, width), BF16),
            pltpu.HBM((rows_here, 128), F32),
        ),
        in_specs=smem(3) + vmem(2) + [anywhere],
        out_specs=(anywhere, anywhere, vmem(1)[0]),
        scratch_shapes=[
            pltpu.VMEM((work, work + halo), BF16),
            pltpu.VMEM((rows_here, width), BF16),
            pltpu.VMEM((work, width), BF16),
            pltpu.SMEM(((work // TILE) * ((work + halo) // TILE),), jnp.int32),
            pltpu.SMEM((slots,), jnp.int32),
            pltpu.SMEM((work // TILE,), jnp.int32),
            pltpu.SMEM((slots,), jnp.int32),
            pltpu.SemaphoreType.DMA,
            pltpu.SemaphoreType.DMA((work // TILE,)),
            pltpu.SemaphoreType.DMA((work // 512,)),
        ],
        compiler_params=params(40),
        cost_estimate=cost(2 * work * rows_here * width, 20 * MIB),
        name="prepare",
    )(tile_rows[0, 0], tile_cols[0, 0], tile_count[0], place, tile_vals[0, 0], cotangent)

    live = jnp.arange(HCAP)[None, :] < halo_count[0, 0][:, None]
    wanted = jnp.where(live, halo_ids[0, 0], -1)
    wanted, place = lax.optimization_barrier((wanted, place))
    wanted = wanted.reshape(size, 2, HCAP)
    wanted = lax.dynamic_slice_in_dim(jnp.concatenate([wanted, wanted]), x, size, axis=0)

    def shift(value, by):
        return lax.ppermute(value, "x", [(i, (i + by) % size) for i in range(size)])

    asked = jnp.stack([wanted[0]] + [shift(wanted[k], k) for k in range(1, size)])
    asked_own = jnp.where(core == 0, asked[:, 0], asked[:, 1])
    asked_other = swap_cores(jnp.where(core == 0, asked[:, 1], asked[:, 0]))
    asked = jnp.stack([asked_own, asked_other]).reshape(halo, 1)
    blocks = pl.pallas_call(
        pick_body,
        out_shape=(jax.ShapeDtypeStruct((4 * HCAP, width), BF16),) * size,
        in_specs=vmem(2),
        out_specs=tuple(vmem(size)),
        compiler_params=params(12),
        cost_estimate=cost(4 * halo * history.shape[1] * width, 2 * MIB),
        name="pick",
    )(jnp.broadcast_to(asked, (halo, 128)), history)
    send_cot, ws, adjacency, blocks = lax.optimization_barrier((send_cot, ws, adjacency, blocks))
    ws_cot = to_owners(send_cot)

    pieces = [blocks[0]] + [shift(blocks[k], size - k) for k in range(1, size)]
    pieces += [swap_cores(piece) for piece in pieces]

    step = 256
    second, mixed, slopes = pl.pallas_call(
        lambda *refs: forward_body(size, *refs),
        out_shape=(
            pltpu.HBM((work, width), BF16),
            pltpu.HBM((2, work, width), BF16),
            pltpu.HBM((2, work, width), F32),
        ),
        in_specs=smem(2) + [anywhere] * (3 + 2 * size),
        out_specs=(anywhere,) * 3,
        scratch_shapes=[
            pltpu.VMEM((work, work + halo), BF16),
            pltpu.VMEM((2, width, width), BF16),
            pltpu.VMEM((work, width), BF16),
            pltpu.VMEM((work + halo, width), BF16),
            pltpu.VMEM((work + halo, width), BF16),
            pltpu.VMEM((2, work, width), BF16),
            pltpu.VMEM((2, work, width), F32),
            pltpu.VMEM((work, width), BF16),
            pltpu.VMEM((step, width), F32),
            pltpu.VMEM((step, width), F32),
            pltpu.SemaphoreType.DMA((5 + 4 * size,)),
            pltpu.SemaphoreType.DMA((2, 3, work // step)),
        ],
        compiler_params=params(56),
        cost_estimate=cost(4 * work * (work + halo + width) * width, 24 * MIB),
        name="forward",
    )(
        x.reshape(1).astype(jnp.int32),
        core.reshape(1).astype(jnp.int32),
        in_hbm(ws),
        weights,
        adjacency,
        *[in_hbm(piece) for piece in pieces],
    )
    second, ws_cot = lax.optimization_barrier((second, ws_cot))
    returned = to_owners(second)

    kept, given = pl.pallas_call(
        backward_body,
        out_shape=(jax.ShapeDtypeStruct((width * width // 128, 128), F32),) * 2,
        in_specs=smem(1) + [anywhere] * 5,
        out_specs=tuple(vmem(2)),
        scratch_shapes=[
            pltpu.VMEM((work, width), BF16),
            pltpu.VMEM((2, width, width), BF16),
            pltpu.VMEM((work, work), BF16),
            pltpu.VMEM((2, work, width), BF16),
            pltpu.VMEM((2, work, width), F32),
            pltpu.VMEM((width, work), BF16),
            pltpu.SemaphoreType.DMA((10,)),
        ],
        compiler_params=params(56),
        cost_estimate=cost(2 * work * (work + 3 * width) * width, 20 * MIB),
        name="backward",
    )(core.reshape(1).astype(jnp.int32), in_hbm(ws_cot), weights, adjacency, mixed, slopes)
    grads = reduce_rows(reduce_rows(kept + swap_cores(given), "x"), "y")
    grads, returned = lax.optimization_barrier((grads, returned))
    second_out = pl.pallas_call(
        collect_body,
        out_shape=jax.ShapeDtypeStruct((rows_here, width), BF16),
        in_specs=vmem(2),
        out_specs=vmem(1)[0],
        compiler_params=params(24),
        cost_estimate=cost(2 * work * rows_here * width, 2 * MIB),
        name="collect",
    )(column, returned)
    mine = jnp.sum(from_all(grads, "z"), axis=0).astype(BF16)
    mine, second_out = lax.optimization_barrier((mine, second_out))
    return (second_out, spread(mine))


def swap_cores(value):
    return lax.ppermute(value, "core", [(0, 1), (1, 0)])


def reduce_rows(kept, axis):
    size = lax.axis_size(axis)
    share = kept.shape[0] // size
    here = lax.axis_index(axis)

    def rows_of(index):
        return lax.dynamic_slice_in_dim(kept, lax.rem(index, size) * share, share, axis=0)

    total = rows_of(here)
    for k in range(1, size):
        total = total + lax.ppermute(
            rows_of(here + k), axis, [(i, (i + k) % size) for i in range(size)]
        )
    return total


def from_all(value, axes):
    value = jnp.broadcast_to(value[None], (lax.axis_size(axes),) + value.shape)
    return lax.all_to_all(value, axes, split_axis=0, concat_axis=0, tiled=True)


def spread(mine):
    parts = from_all(mine, ("x", "y"))
    own = parts.reshape(-1, parts.shape[-1])
    other = swap_cores(own)
    core = lax.axis_index("core")
    both = [jnp.where(core == 0, own, other), jnp.where(core == 0, other, own)]
    rows, lanes = own.shape
    width = math.isqrt(rows * lanes)
    return jnp.stack(
        [
            jnp.concatenate([one[i : i + width] for i in range(0, rows, width)], axis=1)
            for one in both
        ]
    ).astype(F32)


def solution(mesh):
    sizes = (4, mesh.shape["wide"] // 4, mesh.shape["hist"] // 2, 2)
    split = Mesh(mesh.devices.reshape(sizes), WIDE + HIST)
    rows = P(WIDE + HIST, None)
    placed = (
        rows,
        rows,
        rows,
        P(),
        P(None, HIST, None),
        P(WIDE, HIST, None, None),
        P(WIDE, HIST, None),
        P(WIDE, HIST, None),
        P(WIDE, HIST, None),
        P(WIDE, HIST),
        P(WIDE, HIST, None, None, None),
    )
    return jax.shard_map(
        local,
        mesh=split,
        in_specs=placed,
        out_specs=(rows, P()),
        check_vma=False,
    )
```

```python
import math

import jax
import jax.numpy as jnp
from jax import lax
from jax.experimental import pallas as pl
from jax.experimental.pallas import tpu as pltpu
from jax.sharding import Mesh
from jax.sharding import PartitionSpec as P

ALPHA = 0.1
BETAS = (math.log(1.5), math.log(1.25))
TILE = 128
CAP = 64
HCAP = 64
MARK = 1024.0
LIMIT = 512.0
BF16 = jnp.bfloat16
F32 = jnp.float32
MIB = 1 << 20
WIDE = ("y", "z")
HIST = ("x", "core")


def vmem(count):
    return [pl.BlockSpec(memory_space=pltpu.VMEM)] * count


def smem(count):
    return [pl.BlockSpec(memory_space=pltpu.SMEM)] * count


def params(limit):
    return pltpu.CompilerParams(vmem_limit_bytes=limit * MIB)


def cost(flops, moved):
    return pl.CostEstimate(flops=flops, bytes_accessed=moved, transcendentals=0)


def in_hbm(value):
    return pltpu.with_memory_space_constraint(value, pltpu.HBM)


def dot(a, b):
    return jnp.dot(a, b, preferred_element_type=F32)


def dot_rows(a, b):
    return lax.dot_general(a, b, (((0,), (0,)), ((), ())), preferred_element_type=F32)


def hits_of(place, start, step):
    slots = lax.broadcasted_iota(jnp.int32, (step, place.shape[1]), 0) + start
    return (slots == place).astype(F32)


def route_body(n_wide, own_hbm, x_hbm, send_hbm, place_hbm, own_all, place_all, x_all, send, load_sem, send_sem):
    first = pltpu.make_async_copy(own_hbm, own_all, load_sem.at[0])
    first.start()
    load = pltpu.make_async_copy(x_hbm, x_all, load_sem.at[1])
    load.start()
    rows_here = own_all.shape[1]
    blocks = rows_here // 128
    first.wait()
    own = own_all[...]
    hot = (own == lax.broadcasted_iota(jnp.int32, (n_wide, rows_here), 0)).astype(F32)
    hot_b = hot.astype(BF16)
    lower = lax.broadcasted_iota(jnp.int32, (128, 128), 0)
    upper = lax.broadcasted_iota(jnp.int32, (128, 128), 1)
    earlier = (lower < upper).astype(F32).astype(BF16)
    parts = [slice(128 * b, 128 * (b + 1)) for b in range(blocks)]
    inside = dot(jnp.concatenate([hot_b[:, part] for part in parts], axis=0), earlier)
    before = jnp.zeros((n_wide, 1), F32)
    ranks = []
    for b, part in enumerate(parts):
        seen = inside[n_wide * b : n_wide * (b + 1)] + before
        ranks.append(jnp.sum(seen * hot[:, part], axis=0, keepdims=True))
        before = before + jnp.sum(hot[:, part], axis=1, keepdims=True)
    rank = jnp.concatenate(ranks, axis=1)
    place_all[...] = own * CAP + rank.astype(jnp.int32)
    stores = [pltpu.make_async_copy(place_all, place_hbm, load_sem.at[2])]
    stores[0].start()
    by_rank = (rank == lax.broadcasted_iota(jnp.int32, (CAP, rows_here), 0).astype(F32)).astype(F32)
    by_rank = by_rank.astype(BF16)
    slot = lax.broadcasted_iota(jnp.int32, (CAP, 1), 0).astype(F32)
    load.wait()
    peers = 8
    step = peers * CAP
    for c in range(n_wide // peers):
        part = pl.ds(c * step, step)
        group = range(c * peers, (c + 1) * peers)
        hit = jnp.concatenate([by_rank * hot_b[o : o + 1, :] for o in group], axis=0)
        held = jnp.concatenate([slot < before[o : o + 1, :] for o in group], axis=0)
        send[part, :] = jnp.where(held, dot(hit, x_all[...]), MARK).astype(BF16)
        store = pltpu.make_async_copy(send.at[part], send_hbm.at[part], send_sem.at[c])
        store.start()
        stores.append(store)
    for store in stores:
        store.wait()


def prepare_body(
    rows_ref, cols_ref, count_ref, place_ref, vals, cot_hbm, adj_hbm, send_hbm, column_ref,
    adj, cot, send, head, following, row_head, row_next, load_sem, adj_sem, send_sem,
):
    load = pltpu.make_async_copy(cot_hbm, cot, load_sem)
    load.start()
    count = count_ref[0]
    n_rows, wide = adj.shape[0] // TILE, adj.shape[1] // TILE
    for r in range(n_rows):
        row_head[r] = -1

    def clear(k, carry):
        head[rows_ref[k] * wide + cols_ref[k]] = -1
        return carry

    lax.fori_loop(0, count, clear, 0)

    def chain(i, carry):
        k = count - 1 - i
        row = rows_ref[k]
        cell = row * wide + cols_ref[k]
        following[k] = head[cell]
        head[cell] = k
        row_next[k] = row_head[row]
        row_head[row] = k
        return carry

    lax.fori_loop(0, count, chain, 0)

    def row_copy(r):
        part = pl.ds(pl.multiple_of(r * TILE, TILE), TILE)
        return pltpu.make_async_copy(adj.at[part], adj_hbm.at[part], adj_sem.at[r])

    def fill(r, carry):
        part = pl.ds(pl.multiple_of(r * TILE, TILE), TILE)
        adj[part, :] = jnp.zeros((TILE, adj.shape[1]), BF16)

        def place_tile(k):
            col = cols_ref[k]

            @pl.when(head[r * wide + col] == k)
            def _():
                def more(state):
                    at, total = state
                    return following[at], total + vals[at].astype(F32)

                _, total = lax.while_loop(
                    lambda state: state[0] >= 0, more, (following[k], vals[k].astype(F32))
                )
                adj[part, pl.ds(pl.multiple_of(col * TILE, TILE), TILE)] = total.astype(BF16)

            return row_next[k]

        lax.while_loop(lambda k: k >= 0, place_tile, row_head[r])
        row_copy(r).start()
        return carry

    lax.fori_loop(0, n_rows, fill, 0)
    load.wait()
    place = place_ref[...]
    step = 512
    stores = []
    for c in range(send.shape[0] // step):
        part = pl.ds(c * step, step)
        hit = hits_of(place, c * step, step).astype(BF16)
        send[part, :] = dot(hit, cot[...]).astype(BF16)
        store = pltpu.make_async_copy(send.at[part], send_hbm.at[part], send_sem.at[c])
        store.start()
        stores.append(store)
    for b in range(place.shape[1] // 128):
        part = place[:, 128 * b : 128 * (b + 1)].astype(F32)
        column_ref[pl.ds(128 * b, 128), :] = jnp.transpose(jnp.broadcast_to(part, (128, 128)))
    for store in stores:
        store.wait()

    def drain(r, carry):
        row_copy(r).wait()
        return carry

    lax.fori_loop(0, n_rows, drain, 0)


def pick_body(ids_ref, history_ref, *block_refs):
    slots = ids_ref.shape[0]
    here = history_ref.shape[1]
    lane = lax.broadcasted_iota(jnp.int32, (slots, 128), 1)
    ids = ids_ref[...]
    hit = jnp.concatenate(
        [(ids - 128 * c == lane).astype(F32).astype(BF16) for c in range(here // 128)], axis=1
    )
    size = len(block_refs)
    for layer in range(2):
        rows = dot(hit, history_ref[layer]).astype(BF16)
        for side in range(2):
            for k, ref in enumerate(block_refs):
                at = (side * size + k) * HCAP
                ref[pl.ds((2 * side + layer) * HCAP, HCAP), :] = rows[at : at + HCAP]


def forward_body(size, x_ref, core_ref, ws_hbm, w_hbm, adj_hbm, *rest):
    pieces = rest[:size], rest[size : 2 * size]
    out_hbm, m_hbm, s_hbm, adj, w, ws, ext0, ext1, m_all, s_all, out, acc0, acc1, load_sem, keep_sem = rest[2 * size :]
    work, width = ws.shape
    step = acc0.shape[0]
    blocks = work // step
    rows = [pl.ds(b * step, step) for b in range(blocks)]
    x, core = x_ref[0], core_ref[0]
    first = pltpu.make_async_copy(ws_hbm, ws, load_sem.at[0])
    first.start()
    loads = {}

    def load_rows(b, until):
        part = pl.ds(b * step, (until - b) * step)
        sem = load_sem.at[2 + 4 * size + len(loads)]
        loads[b] = pltpu.make_async_copy(adj_hbm.at[part], adj.at[part], sem)
        loads[b].start()

    def load_halo(layer, ext):
        copies = []
        for k in range(size):
            for side in range(2):
                shard = lax.rem(x + k, size) * 2 + lax.rem(core + side, 2)
                there = pl.ds(pl.multiple_of(work + shard * HCAP, HCAP), HCAP)
                here = pl.ds((2 * side + layer) * HCAP, HCAP)
                sem = load_sem.at[2 + (layer * size + k) * 2 + side]
                copies.append(pltpu.make_async_copy(pieces[side][k].at[here], ext.at[there], sem))
                copies[-1].start()
        return copies

    load_rows(0, 1)
    halos = [load_halo(0, ext0)]
    load_rows(1, 4)
    weight = pltpu.make_async_copy(w_hbm, w, load_sem.at[1])
    weight.start()
    load_rows(4, blocks)
    halos.append(load_halo(1, ext1))
    first.wait()
    for part in rows:
        got = ws[part, :].astype(F32)
        ext0[part, :] = jnp.where(got < LIMIT, got, 0.0).astype(BF16)
    for copy in halos[0]:
        copy.wait()
    weight.wait()
    stores = []

    def store(here, there, *at):
        copy = pltpu.make_async_copy(here, there, keep_sem.at[*at])
        copy.start()
        stores.append(copy)

    def keep(layer, b):
        part = rows[b]
        store(m_all.at[layer, part], m_hbm.at[layer, part], layer, 0, b)
        store(s_all.at[layer, part], s_hbm.at[layer, part], layer, 1, b)

    def finish(layer, b, support):
        part = rows[b]
        beta = BETAS[layer]
        mixed = (1.0 - ALPHA) * support + ALPHA * ext0[part, :].astype(F32)
        mixed_b = mixed.astype(BF16)
        m_all[layer, part, :] = mixed_b
        pre = (1.0 - beta) * mixed + beta * dot(mixed_b, w[layer])
        sig = jax.nn.sigmoid(pre)
        valid = ws[part, :].astype(F32) < LIMIT
        raw = pre * sig
        new = jnp.where(valid, raw, 0.0).astype(BF16)
        s_all[layer, part, :] = jnp.where(valid, sig + raw * (1.0 - sig), 0.0)
        (ext1, out)[layer][part, :] = new
        if layer == 1:
            store(out.at[part], out_hbm.at[part], 1, 2, b)
        keep(layer, b)

    accs = (acc0, acc1)
    for layer, ext in enumerate((ext0, ext1)):
        for b in range(blocks + 1):
            if b < blocks:
                if layer == 0 and b in loads:
                    loads[b].wait()
                accs[b % 2][...] = dot(adj[rows[b], :], ext[...])
            if b > 0:
                finish(layer, b - 1, accs[(b - 1) % 2][...])
        if layer == 0:
            for copy in halos[1]:
                copy.wait()
    for copy in stores:
        copy.wait()


def backward_body(core_ref, cot_hbm, w_hbm, adj_hbm, m_hbm, s_hbm, kept_ref, given_ref, cot, w, adj, m_all, s_all, turned, load_sem):
    work, width = cot.shape
    step = 512
    blocks = work // step
    parts = [pl.ds(b * step, step) for b in range(blocks)]
    pairs = [(w_hbm.at[1], w.at[1])]
    for part in parts:
        pairs.append((s_hbm.at[1, part], s_all.at[1, part]))
        pairs.append((cot_hbm.at[part], cot.at[part]))
        pairs.append((m_hbm.at[1, part], m_all.at[1, part]))
    for part in parts:
        pairs.append((adj_hbm.at[:, part], adj.at[:, part]))
        pairs.append((s_hbm.at[0, part], s_all.at[0, part]))
        pairs.append((m_hbm.at[0, part], m_all.at[0, part]))
    loads = [
        pltpu.make_async_copy(here, there, load_sem.at[i]) for i, (here, there) in enumerate(pairs)
    ]
    for load in loads:
        load.start()
    loads[0].wait()
    beta = BETAS[1]
    total = jnp.zeros((width, width), F32)
    for b, part in enumerate(parts):
        for load in loads[1 + 3 * b : 4 + 3 * b]:
            load.wait()
        grad_two = cot[part, :].astype(F32) * s_all[1, part, :]
        grad_two_b = grad_two.astype(BF16)
        total = total + dot_rows(m_all[1, part, :], grad_two_b)
        through = lax.dot_general(
            grad_two_b, w[1], (((1,), (1,)), ((), ())), preferred_element_type=F32
        )
        grad_mix = (1.0 - beta) * grad_two + beta * through
        turned[:, part] = jnp.transpose(grad_mix.astype(BF16))
    second = BETAS[1] * total
    total = jnp.zeros((width, width), F32)
    for b, part in enumerate(parts):
        for load in loads[1 + 3 * (blocks + b) : 4 + 3 * (blocks + b)]:
            load.wait()
        back = jnp.transpose(dot(turned[...], adj[:, part]))
        grad_one = (1.0 - ALPHA) * back * s_all[0, part, :]
        total = total + dot_rows(m_all[0, part, :], grad_one.astype(BF16))
    first = BETAS[0] * total
    lower = core_ref[0] == 0
    for i in range(width // 128):
        here, there = slice(128 * i, 128 * (i + 1)), pl.ds(width * i, width)
        kept_ref[there, :] = jnp.where(lower, first[:, here], second[:, here])
        given_ref[there, :] = jnp.where(lower, second[:, here], first[:, here])


def collect_body(column_ref, back_ref, out_ref):
    slots = back_ref.shape[0]
    step = 256
    lane = lax.broadcasted_iota(jnp.int32, (step, 128), 1).astype(F32)
    for b in range(out_ref.shape[0] // step):
        part = pl.ds(b * step, step)
        place = column_ref[part, :]
        hit = jnp.concatenate(
            [(place - 128.0 * c == lane).astype(F32).astype(BF16) for c in range(slots // 128)],
            axis=1,
        )
        out_ref[part, :] = dot(hit, back_ref[...]).astype(BF16)


def local(
    x_home,
    cotangent,
    owner,
    weights,
    history,
    halo_ids,
    halo_count,
    tile_rows,
    tile_cols,
    tile_count,
    tile_vals,
):
    n_wide = lax.axis_size(WIDE)
    n_hist = lax.axis_size(HIST)
    rows_here, width = x_home.shape
    work = n_wide * CAP
    halo = n_hist * HCAP
    slots = tile_vals.shape[2]

    anywhere = pl.BlockSpec(memory_space=pl.ANY)
    x = lax.axis_index("x")
    core = lax.axis_index("core")
    size = lax.axis_size("x")

    def to_owners(value):
        value = value.reshape(n_wide, CAP, width)
        return lax.all_to_all(value, WIDE, split_axis=0, concat_axis=0, tiled=True).reshape(
            work, width
        )

    send, place = pl.pallas_call(
        lambda *refs: route_body(n_wide, *refs),
        out_shape=(
            pltpu.HBM((work, width), BF16),
            pltpu.HBM((1, rows_here), jnp.int32),
        ),
        in_specs=[anywhere] * 2,
        out_specs=(anywhere,) * 2,
        scratch_shapes=[
            pltpu.VMEM((1, rows_here), jnp.int32),
            pltpu.VMEM((1, rows_here), jnp.int32),
            pltpu.VMEM((rows_here, width), BF16),
            pltpu.VMEM((work, width), BF16),
            pltpu.SemaphoreType.DMA((3,)),
            pltpu.SemaphoreType.DMA((work // 512,)),
        ],
        compiler_params=params(56),
        cost_estimate=cost(2 * work * rows_here * width, 2 * MIB),
        name="route",
    )(owner.reshape(1, rows_here), x_home)
    ws = to_owners(send)

    adjacency, send_cot, column = pl.pallas_call(
        prepare_body,
        out_shape=(
            pltpu.HBM((work, work + halo), BF16),
            pltpu.HBM((work, width), BF16),
            pltpu.HBM((rows_here, 128), F32),
        ),
        in_specs=smem(3) + vmem(2) + [anywhere],
        out_specs=(anywhere, anywhere, vmem(1)[0]),
        scratch_shapes=[
            pltpu.VMEM((work, work + halo), BF16),
            pltpu.VMEM((rows_here, width), BF16),
            pltpu.VMEM((work, width), BF16),
            pltpu.SMEM(((work // TILE) * ((work + halo) // TILE),), jnp.int32),
            pltpu.SMEM((slots,), jnp.int32),
            pltpu.SMEM((work // TILE,), jnp.int32),
            pltpu.SMEM((slots,), jnp.int32),
            pltpu.SemaphoreType.DMA,
            pltpu.SemaphoreType.DMA((work // TILE,)),
            pltpu.SemaphoreType.DMA((work // 512,)),
        ],
        compiler_params=params(40),
        cost_estimate=cost(2 * work * rows_here * width, 20 * MIB),
        name="prepare",
    )(tile_rows[0, 0], tile_cols[0, 0], tile_count[0], place, tile_vals[0, 0], cotangent)

    live = jnp.arange(HCAP)[None, :] < halo_count[0, 0][:, None]
    wanted = jnp.where(live, halo_ids[0, 0], -1)
    wanted, place = lax.optimization_barrier((wanted, place))
    wanted = wanted.reshape(size, 2, HCAP)
    wanted = lax.dynamic_slice_in_dim(jnp.concatenate([wanted, wanted]), x, size, axis=0)

    def shift(value, by):
        return lax.ppermute(value, "x", [(i, (i + by) % size) for i in range(size)])

    asked = jnp.stack([wanted[0]] + [shift(wanted[k], k) for k in range(1, size)])
    asked_own = jnp.where(core == 0, asked[:, 0], asked[:, 1])
    asked_other = swap_cores(jnp.where(core == 0, asked[:, 1], asked[:, 0]))
    asked = jnp.stack([asked_own, asked_other]).reshape(halo, 1)
    blocks = pl.pallas_call(
        pick_body,
        out_shape=(jax.ShapeDtypeStruct((4 * HCAP, width), BF16),) * size,
        in_specs=vmem(2),
        out_specs=tuple(vmem(size)),
        compiler_params=params(12),
        cost_estimate=cost(4 * halo * history.shape[1] * width, 2 * MIB),
        name="pick",
    )(jnp.broadcast_to(asked, (halo, 128)), history)
    send_cot, ws, adjacency, blocks = lax.optimization_barrier((send_cot, ws, adjacency, blocks))
    ws_cot = to_owners(send_cot)

    pieces = [blocks[0]] + [shift(blocks[k], size - k) for k in range(1, size)]
    pieces += [swap_cores(piece) for piece in pieces]

    step = 256
    second, mixed, slopes = pl.pallas_call(
        lambda *refs: forward_body(size, *refs),
        out_shape=(
            pltpu.HBM((work, width), BF16),
            pltpu.HBM((2, work, width), BF16),
            pltpu.HBM((2, work, width), F32),
        ),
        in_specs=smem(2) + [anywhere] * (3 + 2 * size),
        out_specs=(anywhere,) * 3,
        scratch_shapes=[
            pltpu.VMEM((work, work + halo), BF16),
            pltpu.VMEM((2, width, width), BF16),
            pltpu.VMEM((work, width), BF16),
            pltpu.VMEM((work + halo, width), BF16),
            pltpu.VMEM((work + halo, width), BF16),
            pltpu.VMEM((2, work, width), BF16),
            pltpu.VMEM((2, work, width), F32),
            pltpu.VMEM((work, width), BF16),
            pltpu.VMEM((step, width), F32),
            pltpu.VMEM((step, width), F32),
            pltpu.SemaphoreType.DMA((5 + 4 * size,)),
            pltpu.SemaphoreType.DMA((2, 3, work // step)),
        ],
        compiler_params=params(56),
        cost_estimate=cost(4 * work * (work + halo + width) * width, 24 * MIB),
        name="forward",
    )(
        x.reshape(1).astype(jnp.int32),
        core.reshape(1).astype(jnp.int32),
        in_hbm(ws),
        weights,
        adjacency,
        *[in_hbm(piece) for piece in pieces],
    )
    second, ws_cot = lax.optimization_barrier((second, ws_cot))
    returned = to_owners(second)

    kept, given = pl.pallas_call(
        backward_body,
        out_shape=(jax.ShapeDtypeStruct((width * width // 128, 128), F32),) * 2,
        in_specs=smem(1) + [anywhere] * 5,
        out_specs=tuple(vmem(2)),
        scratch_shapes=[
            pltpu.VMEM((work, width), BF16),
            pltpu.VMEM((2, width, width), BF16),
            pltpu.VMEM((work, work), BF16),
            pltpu.VMEM((2, work, width), BF16),
            pltpu.VMEM((2, work, width), F32),
            pltpu.VMEM((width, work), BF16),
            pltpu.SemaphoreType.DMA((25,)),
        ],
        compiler_params=params(56),
        cost_estimate=cost(2 * work * (work + 3 * width) * width, 20 * MIB),
        name="backward",
    )(core.reshape(1).astype(jnp.int32), in_hbm(ws_cot), weights, adjacency, mixed, slopes)
    grads = reduce_rows(reduce_rows(kept + swap_cores(given), "x"), "y")
    grads, returned = lax.optimization_barrier((grads, returned))
    second_out = pl.pallas_call(
        collect_body,
        out_shape=jax.ShapeDtypeStruct((rows_here, width), BF16),
        in_specs=vmem(2),
        out_specs=vmem(1)[0],
        compiler_params=params(24),
        cost_estimate=cost(2 * work * rows_here * width, 2 * MIB),
        name="collect",
    )(column, returned)
    mine = jnp.sum(from_all(grads, "z"), axis=0).astype(BF16)
    mine, second_out = lax.optimization_barrier((mine, second_out))
    return (second_out, spread(mine))


def swap_cores(value):
    return lax.ppermute(value, "core", [(0, 1), (1, 0)])


def reduce_rows(kept, axis):
    size = lax.axis_size(axis)
    share = kept.shape[0] // size
    here = lax.axis_index(axis)

    def rows_of(index):
        return lax.dynamic_slice_in_dim(kept, lax.rem(index, size) * share, share, axis=0)

    total = rows_of(here)
    for k in range(1, size):
        total = total + lax.ppermute(
            rows_of(here + k), axis, [(i, (i + k) % size) for i in range(size)]
        )
    return total


def from_all(value, axes):
    value = jnp.broadcast_to(value[None], (lax.axis_size(axes),) + value.shape)
    return lax.all_to_all(value, axes, split_axis=0, concat_axis=0, tiled=True)


def spread(mine):
    parts = from_all(mine, ("x", "y"))
    own = parts.reshape(-1, parts.shape[-1])
    other = swap_cores(own)
    core = lax.axis_index("core")
    both = [jnp.where(core == 0, own, other), jnp.where(core == 0, other, own)]
    rows, lanes = own.shape
    width = math.isqrt(rows * lanes)
    return jnp.stack(
        [
            jnp.concatenate([one[i : i + width] for i in range(0, rows, width)], axis=1)
            for one in both
        ]
    ).astype(F32)


def solution(mesh):
    sizes = (4, mesh.shape["wide"] // 4, mesh.shape["hist"] // 2, 2)
    split = Mesh(mesh.devices.reshape(sizes), WIDE + HIST)
    rows = P(WIDE + HIST, None)
    placed = (
        rows,
        rows,
        rows,
        P(),
        P(None, HIST, None),
        P(WIDE, HIST, None, None),
        P(WIDE, HIST, None),
        P(WIDE, HIST, None),
        P(WIDE, HIST, None),
        P(WIDE, HIST),
        P(WIDE, HIST, None, None, None),
    )
    return jax.shard_map(
        local,
        mesh=split,
        in_specs=placed,
        out_specs=(rows, P()),
        check_vma=False,
    )
```

```python
import math

import jax
import jax.numpy as jnp
from jax import lax
from jax.experimental import pallas as pl
from jax.experimental.pallas import tpu as pltpu
from jax.sharding import Mesh
from jax.sharding import PartitionSpec as P

ALPHA = 0.1
BETAS = (math.log(1.5), math.log(1.25))
TILE = 128
CAP = 64
HCAP = 64
MARK = 1024.0
LIMIT = 512.0
BF16 = jnp.bfloat16
F32 = jnp.float32
MIB = 1 << 20
WIDE = ("y", "z")
HIST = ("x", "core")


def vmem(count):
    return [pl.BlockSpec(memory_space=pltpu.VMEM)] * count


def smem(count):
    return [pl.BlockSpec(memory_space=pltpu.SMEM)] * count


def params(limit):
    return pltpu.CompilerParams(vmem_limit_bytes=limit * MIB)


def cost(flops, moved):
    return pl.CostEstimate(flops=flops, bytes_accessed=moved, transcendentals=0)


def in_hbm(value):
    return pltpu.with_memory_space_constraint(value, pltpu.HBM)


def dot(a, b):
    return jnp.dot(a, b, preferred_element_type=F32)


def dot_rows(a, b):
    return lax.dot_general(a, b, (((0,), (0,)), ((), ())), preferred_element_type=F32)


def hits_of(place, start, step):
    slots = lax.broadcasted_iota(jnp.int32, (step, place.shape[1]), 0) + start
    return (slots == place).astype(F32)


def route_body(n_wide, own_hbm, x_hbm, send_hbm, place_hbm, own_all, place_all, x_all, send, load_sem, send_sem):
    first = pltpu.make_async_copy(own_hbm, own_all, load_sem.at[0])
    first.start()
    load = pltpu.make_async_copy(x_hbm, x_all, load_sem.at[1])
    load.start()
    rows_here = own_all.shape[1]
    blocks = rows_here // 128
    first.wait()
    own = own_all[...]
    hot = (own == lax.broadcasted_iota(jnp.int32, (n_wide, rows_here), 0)).astype(F32)
    hot_b = hot.astype(BF16)
    lower = lax.broadcasted_iota(jnp.int32, (128, 128), 0)
    upper = lax.broadcasted_iota(jnp.int32, (128, 128), 1)
    earlier = (lower < upper).astype(F32).astype(BF16)
    parts = [slice(128 * b, 128 * (b + 1)) for b in range(blocks)]
    inside = dot(jnp.concatenate([hot_b[:, part] for part in parts], axis=0), earlier)
    before = jnp.zeros((n_wide, 1), F32)
    ranks = []
    for b, part in enumerate(parts):
        seen = inside[n_wide * b : n_wide * (b + 1)] + before
        ranks.append(jnp.sum(seen * hot[:, part], axis=0, keepdims=True))
        before = before + jnp.sum(hot[:, part], axis=1, keepdims=True)
    rank = jnp.concatenate(ranks, axis=1)
    place_all[...] = own * CAP + rank.astype(jnp.int32)
    stores = [pltpu.make_async_copy(place_all, place_hbm, load_sem.at[2])]
    stores[0].start()
    by_rank = (rank == lax.broadcasted_iota(jnp.int32, (CAP, rows_here), 0).astype(F32)).astype(F32)
    by_rank = by_rank.astype(BF16)
    slot = lax.broadcasted_iota(jnp.int32, (CAP, 1), 0).astype(F32)
    load.wait()
    peers = 8
    step = peers * CAP
    for c in range(n_wide // peers):
        part = pl.ds(c * step, step)
        group = range(c * peers, (c + 1) * peers)
        hit = jnp.concatenate([by_rank * hot_b[o : o + 1, :] for o in group], axis=0)
        held = jnp.concatenate([slot < before[o : o + 1, :] for o in group], axis=0)
        send[part, :] = jnp.where(held, dot(hit, x_all[...]), MARK).astype(BF16)
        store = pltpu.make_async_copy(send.at[part], send_hbm.at[part], send_sem.at[c])
        store.start()
        stores.append(store)
    for store in stores:
        store.wait()


def prepare_body(
    rows_ref, cols_ref, count_ref, place_ref, vals, cot_hbm, adj_hbm, send_hbm, column_ref,
    adj, cot, send, head, following, row_head, row_next, load_sem, adj_sem, send_sem,
):
    load = pltpu.make_async_copy(cot_hbm, cot, load_sem)
    load.start()
    count = count_ref[0]
    n_rows, wide = adj.shape[0] // TILE, adj.shape[1] // TILE
    for r in range(n_rows):
        row_head[r] = -1

    def clear(k, carry):
        head[rows_ref[k] * wide + cols_ref[k]] = -1
        return carry

    lax.fori_loop(0, count, clear, 0)

    def chain(i, carry):
        k = count - 1 - i
        row = rows_ref[k]
        cell = row * wide + cols_ref[k]
        following[k] = head[cell]
        head[cell] = k
        row_next[k] = row_head[row]
        row_head[row] = k
        return carry

    lax.fori_loop(0, count, chain, 0)

    def row_copy(r):
        part = pl.ds(pl.multiple_of(r * TILE, TILE), TILE)
        return pltpu.make_async_copy(adj.at[part], adj_hbm.at[part], adj_sem.at[r])

    def fill(r, carry):
        part = pl.ds(pl.multiple_of(r * TILE, TILE), TILE)
        adj[part, :] = jnp.zeros((TILE, adj.shape[1]), BF16)

        def place_tile(k):
            col = cols_ref[k]

            @pl.when(head[r * wide + col] == k)
            def _():
                def more(state):
                    at, total = state
                    return following[at], total + vals[at].astype(F32)

                _, total = lax.while_loop(
                    lambda state: state[0] >= 0, more, (following[k], vals[k].astype(F32))
                )
                adj[part, pl.ds(pl.multiple_of(col * TILE, TILE), TILE)] = total.astype(BF16)

            return row_next[k]

        lax.while_loop(lambda k: k >= 0, place_tile, row_head[r])
        row_copy(r).start()
        return carry

    lax.fori_loop(0, n_rows, fill, 0)
    load.wait()
    place = place_ref[...]
    step = 512
    stores = []
    for c in range(send.shape[0] // step):
        part = pl.ds(c * step, step)
        hit = hits_of(place, c * step, step).astype(BF16)
        send[part, :] = dot(hit, cot[...]).astype(BF16)
        store = pltpu.make_async_copy(send.at[part], send_hbm.at[part], send_sem.at[c])
        store.start()
        stores.append(store)
    for b in range(place.shape[1] // 128):
        part = place[:, 128 * b : 128 * (b + 1)].astype(F32)
        column_ref[pl.ds(128 * b, 128), :] = jnp.transpose(jnp.broadcast_to(part, (128, 128)))
    for store in stores:
        store.wait()

    def drain(r, carry):
        row_copy(r).wait()
        return carry

    lax.fori_loop(0, n_rows, drain, 0)


def pick_body(ids_ref, history_ref, *block_refs):
    slots = ids_ref.shape[0]
    here = history_ref.shape[1]
    lane = lax.broadcasted_iota(jnp.int32, (slots, 128), 1)
    ids = ids_ref[...]
    hit = jnp.concatenate(
        [(ids - 128 * c == lane).astype(F32).astype(BF16) for c in range(here // 128)], axis=1
    )
    size = len(block_refs)
    for layer in range(2):
        rows = dot(hit, history_ref[layer]).astype(BF16)
        for side in range(2):
            for k, ref in enumerate(block_refs):
                at = (side * size + k) * HCAP
                ref[pl.ds((2 * side + layer) * HCAP, HCAP), :] = rows[at : at + HCAP]


def forward_body(size, x_ref, core_ref, ws_hbm, w_hbm, adj_hbm, *rest):
    pieces = rest[:size], rest[size : 2 * size]
    out_hbm, m_hbm, s_hbm, adj, w, ws, ext0, ext1, m_all, s_all, out, acc0, acc1, load_sem, keep_sem = rest[2 * size :]
    work, width = ws.shape
    step = acc0.shape[0]
    blocks = work // step
    rows = [pl.ds(b * step, step) for b in range(blocks)]
    x, core = x_ref[0], core_ref[0]
    first = pltpu.make_async_copy(ws_hbm, ws, load_sem.at[0])
    first.start()
    loads = {}

    def load_rows(b, until):
        part = pl.ds(b * step, (until - b) * step)
        sem = load_sem.at[2 + 4 * size + len(loads)]
        loads[b] = pltpu.make_async_copy(adj_hbm.at[part], adj.at[part], sem)
        loads[b].start()

    def load_halo(layer, ext):
        copies = []
        for k in range(size):
            for side in range(2):
                shard = lax.rem(x + k, size) * 2 + lax.rem(core + side, 2)
                there = pl.ds(pl.multiple_of(work + shard * HCAP, HCAP), HCAP)
                here = pl.ds((2 * side + layer) * HCAP, HCAP)
                sem = load_sem.at[2 + (layer * size + k) * 2 + side]
                copies.append(pltpu.make_async_copy(pieces[side][k].at[here], ext.at[there], sem))
                copies[-1].start()
        return copies

    load_rows(0, 1)
    halos = [load_halo(0, ext0)]
    load_rows(1, 4)
    weight = pltpu.make_async_copy(w_hbm, w, load_sem.at[1])
    weight.start()
    load_rows(4, blocks)
    halos.append(load_halo(1, ext1))
    first.wait()
    for part in rows:
        got = ws[part, :].astype(F32)
        ext0[part, :] = jnp.where(got < LIMIT, got, 0.0).astype(BF16)
    for copy in halos[0]:
        copy.wait()
    weight.wait()
    stores = []

    def store(here, there, *at):
        copy = pltpu.make_async_copy(here, there, keep_sem.at[*at])
        copy.start()
        stores.append(copy)

    def keep(layer, b):
        part = rows[b]
        store(m_all.at[layer, part], m_hbm.at[layer, part], layer, 0, b)
        store(s_all.at[layer, part], s_hbm.at[layer, part], layer, 1, b)

    def finish(layer, b, support):
        part = rows[b]
        beta = BETAS[layer]
        mixed = (1.0 - ALPHA) * support + ALPHA * ext0[part, :].astype(F32)
        mixed_b = mixed.astype(BF16)
        m_all[layer, part, :] = mixed_b
        pre = (1.0 - beta) * mixed + beta * dot(mixed_b, w[layer])
        sig = jax.nn.sigmoid(pre)
        valid = ws[part, :].astype(F32) < LIMIT
        raw = pre * sig
        new = jnp.where(valid, raw, 0.0).astype(BF16)
        s_all[layer, part, :] = jnp.where(valid, sig + raw * (1.0 - sig), 0.0)
        (ext1, out)[layer][part, :] = new
        if layer == 1:
            store(out.at[part], out_hbm.at[part], 1, 2, b)
        keep(layer, b)

    accs = (acc0, acc1)
    for layer, ext in enumerate((ext0, ext1)):
        for b in range(blocks + 1):
            if b < blocks:
                if layer == 0 and b in loads:
                    loads[b].wait()
                accs[b % 2][...] = dot(adj[rows[b], :], ext[...])
            if b > 0:
                finish(layer, b - 1, accs[(b - 1) % 2][...])
        if layer == 0:
            for copy in halos[1]:
                copy.wait()
    for copy in stores:
        copy.wait()


def backward_body(core_ref, cot_hbm, w_hbm, adj_hbm, m_hbm, s_hbm, kept_ref, given_ref, cot, w, adj, m_all, s_all, turned, load_sem):
    work, width = cot.shape
    step = 512
    blocks = work // step
    parts = [pl.ds(b * step, step) for b in range(blocks)]
    pairs = [(w_hbm.at[1], w.at[1])]
    for part in parts:
        pairs.append((s_hbm.at[1, part], s_all.at[1, part]))
        pairs.append((cot_hbm.at[part], cot.at[part]))
        pairs.append((m_hbm.at[1, part], m_all.at[1, part]))
    for part in parts:
        pairs.append((adj_hbm.at[:, part], adj.at[:, part]))
        pairs.append((s_hbm.at[0, part], s_all.at[0, part]))
        pairs.append((m_hbm.at[0, part], m_all.at[0, part]))
    loads = [
        pltpu.make_async_copy(here, there, load_sem.at[i]) for i, (here, there) in enumerate(pairs)
    ]
    for load in loads:
        load.start()
    loads[0].wait()
    beta = BETAS[1]
    total = jnp.zeros((width, width), F32)
    for b, part in enumerate(parts):
        for load in loads[1 + 3 * b : 4 + 3 * b]:
            load.wait()
        grad_two = cot[part, :].astype(F32) * s_all[1, part, :]
        grad_two_b = grad_two.astype(BF16)
        total = total + dot_rows(m_all[1, part, :], grad_two_b)
        through = lax.dot_general(
            grad_two_b, w[1], (((1,), (1,)), ((), ())), preferred_element_type=F32
        )
        grad_mix = (1.0 - beta) * grad_two + beta * through
        turned[:, part] = jnp.transpose(grad_mix.astype(BF16))
    second = BETAS[1] * total
    total = jnp.zeros((width, width), F32)
    for b, part in enumerate(parts):
        for load in loads[1 + 3 * (blocks + b) : 4 + 3 * (blocks + b)]:
            load.wait()
        back = jnp.transpose(dot(turned[...], adj[:, part]))
        grad_one = (1.0 - ALPHA) * back * s_all[0, part, :]
        total = total + dot_rows(m_all[0, part, :], grad_one.astype(BF16))
    first = BETAS[0] * total
    lower = core_ref[0] == 0
    for i in range(width // 128):
        here, there = slice(128 * i, 128 * (i + 1)), pl.ds(width * i, width)
        kept_ref[there, :] = jnp.where(lower, first[:, here], second[:, here])
        given_ref[there, :] = jnp.where(lower, second[:, here], first[:, here])


def collect_body(column_ref, back_ref, out_ref):
    slots = back_ref.shape[0]
    step = 256
    lane = lax.broadcasted_iota(jnp.int32, (step, 128), 1).astype(F32)
    for b in range(out_ref.shape[0] // step):
        part = pl.ds(b * step, step)
        place = column_ref[part, :]
        hit = jnp.concatenate(
            [(place - 128.0 * c == lane).astype(F32).astype(BF16) for c in range(slots // 128)],
            axis=1,
        )
        out_ref[part, :] = dot(hit, back_ref[...]).astype(BF16)


def local(
    x_home,
    cotangent,
    owner,
    weights,
    history,
    halo_ids,
    halo_count,
    tile_rows,
    tile_cols,
    tile_count,
    tile_vals,
):
    n_wide = lax.axis_size(WIDE)
    n_hist = lax.axis_size(HIST)
    rows_here, width = x_home.shape
    work = n_wide * CAP
    halo = n_hist * HCAP
    slots = tile_vals.shape[2]

    anywhere = pl.BlockSpec(memory_space=pl.ANY)
    x = lax.axis_index("x")
    core = lax.axis_index("core")
    size = lax.axis_size("x")

    def to_owners(value):
        value = value.reshape(n_wide, CAP, width)
        return lax.all_to_all(value, WIDE, split_axis=0, concat_axis=0, tiled=True).reshape(
            work, width
        )

    send, place = pl.pallas_call(
        lambda *refs: route_body(n_wide, *refs),
        out_shape=(
            pltpu.HBM((work, width), BF16),
            pltpu.HBM((1, rows_here), jnp.int32),
        ),
        in_specs=[anywhere] * 2,
        out_specs=(anywhere,) * 2,
        scratch_shapes=[
            pltpu.VMEM((1, rows_here), jnp.int32),
            pltpu.VMEM((1, rows_here), jnp.int32),
            pltpu.VMEM((rows_here, width), BF16),
            pltpu.VMEM((work, width), BF16),
            pltpu.SemaphoreType.DMA((3,)),
            pltpu.SemaphoreType.DMA((work // 512,)),
        ],
        compiler_params=params(56),
        cost_estimate=cost(2 * work * rows_here * width, 2 * MIB),
        name="route",
    )(owner.reshape(1, rows_here), x_home)
    ws = to_owners(send)

    adjacency, send_cot, column = pl.pallas_call(
        prepare_body,
        out_shape=(
            pltpu.HBM((work, work + halo), BF16),
            pltpu.HBM((work, width), BF16),
            pltpu.HBM((rows_here, 128), F32),
        ),
        in_specs=smem(3) + vmem(2) + [anywhere],
        out_specs=(anywhere, anywhere, vmem(1)[0]),
        scratch_shapes=[
            pltpu.VMEM((work, work + halo), BF16),
            pltpu.VMEM((rows_here, width), BF16),
            pltpu.VMEM((work, width), BF16),
            pltpu.SMEM(((work // TILE) * ((work + halo) // TILE),), jnp.int32),
            pltpu.SMEM((slots,), jnp.int32),
            pltpu.SMEM((work // TILE,), jnp.int32),
            pltpu.SMEM((slots,), jnp.int32),
            pltpu.SemaphoreType.DMA,
            pltpu.SemaphoreType.DMA((work // TILE,)),
            pltpu.SemaphoreType.DMA((work // 512,)),
        ],
        compiler_params=params(40),
        cost_estimate=cost(2 * work * rows_here * width, 20 * MIB),
        name="prepare",
    )(tile_rows[0, 0], tile_cols[0, 0], tile_count[0], place, tile_vals[0, 0], cotangent)

    live = jnp.arange(HCAP)[None, :] < halo_count[0, 0][:, None]
    wanted = jnp.where(live, halo_ids[0, 0], -1)
    wanted, place = lax.optimization_barrier((wanted, place))
    wanted = wanted.reshape(size, 2, HCAP)
    wanted = lax.dynamic_slice_in_dim(jnp.concatenate([wanted, wanted]), x, size, axis=0)

    def shift(value, by):
        return lax.ppermute(value, "x", [(i, (i + by) % size) for i in range(size)])

    asked = jnp.stack([wanted[0]] + [shift(wanted[k], k) for k in range(1, size)])
    asked_own = jnp.where(core == 0, asked[:, 0], asked[:, 1])
    asked_other = swap_cores(jnp.where(core == 0, asked[:, 1], asked[:, 0]))
    asked = jnp.stack([asked_own, asked_other]).reshape(halo, 1)
    blocks = pl.pallas_call(
        pick_body,
        out_shape=(jax.ShapeDtypeStruct((4 * HCAP, width), BF16),) * size,
        in_specs=vmem(2),
        out_specs=tuple(vmem(size)),
        compiler_params=params(12),
        cost_estimate=cost(4 * halo * history.shape[1] * width, 2 * MIB),
        name="pick",
    )(jnp.broadcast_to(asked, (halo, 128)), history)
    send_cot, ws, adjacency, blocks = lax.optimization_barrier((send_cot, ws, adjacency, blocks))
    ws_cot = to_owners(send_cot)

    pieces = [blocks[0]] + [shift(blocks[k], size - k) for k in range(1, size)]
    pieces += [swap_cores(piece) for piece in pieces]

    step = 256
    second, mixed, slopes = pl.pallas_call(
        lambda *refs: forward_body(size, *refs),
        out_shape=(
            pltpu.HBM((work, width), BF16),
            pltpu.HBM((2, work, width), BF16),
            pltpu.HBM((2, work, width), F32),
        ),
        in_specs=smem(2) + [anywhere] * (3 + 2 * size),
        out_specs=(anywhere,) * 3,
        scratch_shapes=[
            pltpu.VMEM((work, work + halo), BF16),
            pltpu.VMEM((2, width, width), BF16),
            pltpu.VMEM((work, width), BF16),
            pltpu.VMEM((work + halo, width), BF16),
            pltpu.VMEM((work + halo, width), BF16),
            pltpu.VMEM((2, work, width), BF16),
            pltpu.VMEM((2, work, width), F32),
            pltpu.VMEM((work, width), BF16),
            pltpu.VMEM((step, width), F32),
            pltpu.VMEM((step, width), F32),
            pltpu.SemaphoreType.DMA((5 + 4 * size,)),
            pltpu.SemaphoreType.DMA((2, 3, work // step)),
        ],
        compiler_params=params(56),
        cost_estimate=cost(4 * work * (work + halo + width) * width, 24 * MIB),
        name="forward",
    )(
        x.reshape(1).astype(jnp.int32),
        core.reshape(1).astype(jnp.int32),
        in_hbm(ws),
        weights,
        adjacency,
        *[in_hbm(piece) for piece in pieces],
    )
    second, ws_cot = lax.optimization_barrier((second, ws_cot))
    returned = to_owners(second)

    kept, given = pl.pallas_call(
        backward_body,
        out_shape=(jax.ShapeDtypeStruct((width * width // 128, 128), F32),) * 2,
        in_specs=smem(1) + [anywhere] * 5,
        out_specs=tuple(vmem(2)),
        scratch_shapes=[
            pltpu.VMEM((work, width), BF16),
            pltpu.VMEM((2, width, width), BF16),
            pltpu.VMEM((work, work), BF16),
            pltpu.VMEM((2, work, width), BF16),
            pltpu.VMEM((2, work, width), F32),
            pltpu.VMEM((width, work), BF16),
            pltpu.SemaphoreType.DMA((25,)),
        ],
        compiler_params=params(56),
        cost_estimate=cost(2 * work * (work + 3 * width) * width, 20 * MIB),
        name="backward",
    )(core.reshape(1).astype(jnp.int32), in_hbm(ws_cot), weights, adjacency, mixed, slopes)
    grads = sum(reduce_rows(reduce_rows([kept, swap_cores(given)], "x"), "y"))
    grads, returned = lax.optimization_barrier((grads, returned))
    second_out = pl.pallas_call(
        collect_body,
        out_shape=jax.ShapeDtypeStruct((rows_here, width), BF16),
        in_specs=vmem(2),
        out_specs=vmem(1)[0],
        compiler_params=params(24),
        cost_estimate=cost(2 * work * rows_here * width, 2 * MIB),
        name="collect",
    )(column, returned)
    mine = jnp.sum(from_all(grads, "z"), axis=0).astype(BF16)
    mine, second_out = lax.optimization_barrier((mine, second_out))
    return (second_out, spread(mine))


def swap_cores(value):
    return lax.ppermute(value, "core", [(0, 1), (1, 0)])


def reduce_rows(terms, axis):
    size = lax.axis_size(axis)
    share = terms[0].shape[0] // size
    here = lax.axis_index(axis)

    def rows_of(index):
        start = lax.rem(index, size) * share
        return sum(lax.dynamic_slice_in_dim(term, start, share, axis=0) for term in terms)

    shares = [rows_of(here)]
    for k in range(1, size):
        shares.append(
            lax.ppermute(rows_of(here + k), axis, [(i, (i + k) % size) for i in range(size)])
        )
    return shares


def from_all(value, axes):
    value = jnp.broadcast_to(value[None], (lax.axis_size(axes),) + value.shape)
    return lax.all_to_all(value, axes, split_axis=0, concat_axis=0, tiled=True)


def spread(mine):
    parts = from_all(mine, ("x", "y"))
    own = parts.reshape(-1, parts.shape[-1])
    other = swap_cores(own)
    core = lax.axis_index("core")
    both = [jnp.where(core == 0, own, other), jnp.where(core == 0, other, own)]
    rows, lanes = own.shape
    width = math.isqrt(rows * lanes)
    return jnp.stack(
        [
            jnp.concatenate([one[i : i + width] for i in range(0, rows, width)], axis=1)
            for one in both
        ]
    ).astype(F32)


def solution(mesh):
    sizes = (4, mesh.shape["wide"] // 4, mesh.shape["hist"] // 2, 2)
    split = Mesh(mesh.devices.reshape(sizes), WIDE + HIST)
    rows = P(WIDE + HIST, None)
    placed = (
        rows,
        rows,
        rows,
        P(),
        P(None, HIST, None),
        P(WIDE, HIST, None, None),
        P(WIDE, HIST, None),
        P(WIDE, HIST, None),
        P(WIDE, HIST, None),
        P(WIDE, HIST),
        P(WIDE, HIST, None, None, None),
    )
    return jax.shard_map(
        local,
        mesh=split,
        in_specs=placed,
        out_specs=(rows, P()),
        check_vma=False,
    )
```
